32 devices in a mesh: row: 8 (over y, x, core), col: 4 (over z).
Axes of the slice: x: 2, y: 2, z: 4, core: 2. Of those that a mesh axis runs over, the one named last changes fastest.
Arguments:
- features: bfloat16 [32, 1024, 1024], P(None, 'row', 'col'), may hold values from -45 to 45
- first_kernel: bfloat16 [3, 3, 32, 32], replicated, may hold values from -0.375 to 0.375
- second_kernel: bfloat16 [3, 3, 32, 32], replicated, may hold values from -0.375 to 0.375
- first_gain: float32 [32], replicated, may hold values from 0.5 to 1.5
- first_shift: float32 [32], replicated, may hold values from -3 to 3
- second_gain: float32 [32], replicated, may hold values from 0.5 to 1.5
- second_shift: float32 [32], replicated, may hold values from -3 to 3
Outputs:
- symmetric_map: bfloat16 [32, 1024, 1024], P(None, 'row', 'col')
The draws below stay inside these ranges and needn't reach their ends.
All inputs are finite; a program needn't handle non-finite values.
Results may differ from the reference program's by a relative error of at most 0.0053.
Values may be sent and summed in bfloat16 or wider, within the bound.
A program may use at most 192 MiB of HBM per device.

```python
import jax
import jax.numpy as jnp
from jax import lax

C = 32
DILATION_STEP = 8
TILE = 128
SIDE = 1024


def draw_features(key, part):
    noise_key = jax.random.fold_in(key, 11)
    band_key = jax.random.fold_in(key, 37)
    across_key = jax.random.fold_in(key, 41)
    offset_key = jax.random.fold_in(key, 53)
    lateral_key = jax.random.fold_in(key, 67)
    band_len = max(TILE // 2, 1)
    band_count = SIDE // band_len
    row_pos = jnp.arange(SIDE, dtype=jnp.float32)
    col_pos = jnp.arange(SIDE, dtype=jnp.float32)
    row_scale = jnp.repeat(jnp.exp(jax.random.uniform(band_key, (band_count,), jnp.float32, -2.3, 1.1)), band_len)
    col_scale = jnp.repeat(jnp.exp(jax.random.uniform(across_key, (band_count,), jnp.float32, -1.2, 1.2)), band_len)
    row_offset = jnp.repeat(jax.random.uniform(offset_key, (band_count,), jnp.float32, -3.0, 3.0), band_len)
    col_offset = jnp.repeat(jax.random.uniform(lateral_key, (band_count,), jnp.float32, -1.5, 1.5), band_len)
    base = jax.random.truncated_normal(noise_key, -4.0, 4.0, (C, SIDE, SIDE), jnp.float32)
    trend = 1.0 + 2.0 * (row_pos[:, None] + col_pos[None, :]) / (2.0 * SIDE - 2.0)
    decay = 0.5 + jnp.exp(-jnp.abs(row_pos[:, None] - col_pos[None, :]) / (SIDE / 8.0))
    band_scale = row_scale[:, None] * col_scale[None, :]
    band_shift = row_offset[:, None] + col_offset[None, :]
    value = 0.5 * base * (trend * decay * band_scale)[None] + band_shift[None]
    return jnp.clip(value, -45.0, 45.0).astype(jnp.bfloat16)


def gaussian(rng, shape, scale, bound, held_as=jnp.bfloat16):
    drawn = jax.random.normal(rng, shape, jnp.float32) * scale
    return jnp.minimum(jnp.maximum(drawn, -bound), bound).astype(held_as)


def setup_inputs(seed: int = 0) -> dict:
    streams_of = jax.random.split(jax.random.key(seed), 8)
    features = draw_features(jax.random.fold_in(streams_of[7], 71), 0)
    first_kernel = gaussian(streams_of[1], (3, 3, C, C), (9 * C) ** -0.5, 0.375)
    second_kernel = gaussian(streams_of[2], (3, 3, C, C), (9 * C) ** -0.5, 0.375)
    first_gain = jnp.clip(1.0 + 0.1 * jax.random.normal(streams_of[3], (C,), jnp.float32), 0.5, 1.5)
    first_shift = gaussian(streams_of[4], (C,), 0.3, 3.0, jnp.float32)
    second_gain = jnp.clip(1.0 + 0.1 * jax.random.normal(streams_of[5], (C,), jnp.float32), 0.5, 1.5)
    second_shift = gaussian(streams_of[6], (C,), 0.3, 3.0, jnp.float32)
    return dict(features=features, first_kernel=first_kernel, second_kernel=second_kernel, first_gain=first_gain, first_shift=first_shift, second_gain=second_gain, second_shift=second_shift)


epsilon = 1e-05

def dilated(receptive_field, filter_weight):
    block_output = lax.conv_general_dilated(receptive_field[None], filter_weight, (1, 1), ((DILATION_STEP, DILATION_STEP), (DILATION_STEP, DILATION_STEP)), rhs_dilation=(DILATION_STEP, DILATION_STEP), dimension_numbers=('NCHW', 'HWOI', 'NCHW'), preferred_element_type=jnp.float32)
    return block_output[0]

def normalized(hidden, gain, shift):
    centre = lax.optimization_barrier(jnp.mean(hidden, axis=(1, 2)))
    centered = hidden - centre[:, None, None]
    spread = lax.optimization_barrier(jnp.mean(centered * centered, axis=(1, 2)))
    factor = gain.astype(jnp.float32) * lax.rsqrt(spread + epsilon)
    return centered * factor[:, None, None] + shift.astype(jnp.float32)[:, None, None]

def reference(features, first_kernel, second_kernel, first_gain, first_shift, second_gain, second_shift):
    first = dilated(features, first_kernel)
    active = jnp.maximum(normalized(first, first_gain, first_shift), 0.0).astype(jnp.bfloat16)
    second = dilated(active, second_kernel)
    summed = (features.astype(jnp.float32) + normalized(second, second_gain, second_shift)).astype(jnp.bfloat16)
    mirrored = jnp.swapaxes(summed, 1, 2)
    return ((summed.astype(jnp.float32) + mirrored.astype(jnp.float32)) * 0.5).astype(jnp.bfloat16)
```

```python
import functools

import jax
import jax.numpy as jnp
from jax import lax
from jax.experimental import pallas as pl
from jax.experimental.pallas import tpu as pltpu
from jax.sharding import PartitionSpec as P

STEP = 8
GROUP = 4
EPSILON = 1e-05
LANES = 128
PART = 16
MESH = pl.DeviceIdType.MESH
BF16 = jnp.bfloat16
F32 = jnp.float32

DIRECT = ((0, 1), (0, 2), (1, 3), (2, 0), (3, 1), (3, 2))

WAYS = ((-1, -1), (-1, 0), (-1, 1), (0, -1), (0, 1), (1, -1), (1, 0), (1, 1))


def iota(shape, dim):
    return lax.broadcasted_iota(jnp.int32, shape, dim)


def one_hot(mask):
    return jnp.where(mask, 1.0, 0.0).astype(BF16)


def dot(a, b):
    return jnp.dot(a, b, preferred_element_type=F32)


def remote(src, dst, send, recv, device):
    return pltpu.make_async_remote_copy(
        src_ref=src,
        dst_ref=dst,
        send_sem=send,
        recv_sem=recv,
        device_id=device,
        device_id_type=MESH,
    )


def kernel(
    rows,
    cols,
    x_ref,
    first_ref,
    second_ref,
    gain_one,
    shift_one,
    gain_two,
    shift_two,
    out_ref,
    pad_one,
    pad_two,
    hidden,
    pack_sel,
    unpack_sel,
    weights,
    packed,
    strips,
    col_stats,
    row_stats,
    summed,
    got,
    wide,
    relay,
    halo_send,
    halo_recv,
    cs_send,
    cs_recv,
    rs_send,
    rs_recv,
    send,
    recv,
    relay_send,
    relay_recv,
):
    row = lax.axis_index("row")
    col = lax.axis_index("col")
    phases, depth, width = x_ref.shape
    chans, height, _ = out_ref.shape
    count = depth // chans
    full = depth + 2 * chans
    fold_rows = depth // 2
    half_lanes = LANES // 2
    cells = float(phases * count * width)
    centre = pl.ds(LANES, width)
    ratio = rows // cols
    block = lax.div(row, ratio)
    part = lax.rem(row, ratio)
    relays = block == col
    parts = chans // PART
    pieces = parts * phases

    for pad in (pad_one, pad_two):
        pad[:, pl.ds(0, chans), :] = jnp.zeros((phases, chans, width + 2 * LANES), BF16)
        pad[:, pl.ds(depth + chans, chans), :] = jnp.zeros(
            (phases, chans, width + 2 * LANES), BF16
        )
    strips[...] = jnp.zeros_like(strips)

    barrier = pltpu.get_barrier_semaphore()

    def greet(device):
        pl.semaphore_signal(barrier, inc=1, device_id=device, device_id_type=MESH)

    def neighbour(k):
        dr, dc = WAYS[k]
        there = jnp.bool_(True)
        if dr:
            there = there & ((row > 0) if dr < 0 else (row < rows - 1))
        if dc:
            there = there & ((col > 0) if dc < 0 else (col < cols - 1))
        device = (jnp.clip(row + dr, 0, rows - 1), jnp.clip(col + dc, 0, cols - 1))
        return there, device

    expected = jnp.int32(rows + cols - 2)
    for d in range(1, cols):
        greet((row, lax.rem(col + d, cols)))
    for d in range(1, rows):
        greet((lax.rem(row + d, rows), col))
    for k in (0, 2, 5, 7):
        there, device = neighbour(k)
        pl.when(there)(functools.partial(greet, device))
        expected = expected + jnp.where(there, 1, 0)
    for h in range(ratio):
        pl.when(jnp.logical_not(relays))(functools.partial(greet, (ratio * col + h, block)))
    expected = expected + jnp.where(relays, 0, ratio)

    pad_one[:, pl.ds(chans, depth), centre] = x_ref[...]

    i, j = iota((2 * LANES, LANES), 0), iota((2 * LANES, LANES), 1)
    in_half, source_lane = i // LANES, i % LANES
    edge = LANES - STEP
    for phase in range(phases):
        at = in_half * half_lanes + phase * STEP
        pack_sel[phase] = one_hot((source_lane < STEP) & (j == source_lane + at))
        pack_sel[phases + phase] = one_hot((source_lane >= edge) & (j == source_lane - edge + at))
    i, j = iota((LANES, 2 * LANES), 0), iota((LANES, 2 * LANES), 1)
    in_half, target_lane = j // LANES, j % LANES
    for phase in range(phases):
        at = in_half * half_lanes + phase * STEP
        unpack_sel[phase] = one_hot((target_lane >= edge) & (i == target_lane - edge + at))
        unpack_sel[phases + phase] = one_hot((target_lane < STEP) & (i == target_lane + at))

    def band(n, kernel_ref):
        span = (GROUP + 2) * chans
        c, k = iota((chans, span), 0), iota((chans, span), 1)
        for q in range(GROUP):
            for b in range(3):
                total = jnp.zeros((chans, span), F32)
                for a in range(3):
                    total += dot(kernel_ref[a, b], one_hot(k == c + (q + a) * chans))
                weights[n, b, pl.ds(q * chans, chans), :] = total.astype(BF16)

    pl.semaphore_wait(barrier, expected)

    def halo_copy(pad, n, k):
        dr, dc = WAYS[k]
        there, device = neighbour(k)
        if dc == 0:
            source = chans if dr < 0 else depth
            target = depth + chans if dr < 0 else 0
            src = pad.at[:, pl.ds(source, chans), centre]
            dst = pad.at[:, pl.ds(target, chans), centre]
        else:
            mine, theirs = (0, 1) if dc < 0 else (1, 0)
            if dr == 0:
                src = packed.at[n, mine]
                dst = strips.at[n, theirs, pl.ds(0, fold_rows)]
            elif dr < 0:
                src = packed.at[n, mine, pl.ds(0, chans)]
                dst = strips.at[n, theirs, pl.ds(fold_rows + chans, chans)]
            else:
                src = packed.at[n, mine, pl.ds(fold_rows - chans, chans)]
                dst = strips.at[n, theirs, pl.ds(fold_rows, chans)]
        slot = n * 8 + k
        return there, remote(src, dst, halo_send.at[slot], halo_recv.at[slot], device)

    def halo_start(pad, n):
        for k in (1, 6):
            there, copy = halo_copy(pad, n, k)
            pl.when(there)(copy.start)
        for side, lane in ((0, LANES), (1, width)):
            total = jnp.zeros((fold_rows, LANES), F32)
            for phase in range(phases):
                low = pad[phase, pl.ds(chans, fold_rows), pl.ds(lane, LANES)]
                high = pad[phase, pl.ds(chans + fold_rows, fold_rows), pl.ds(lane, LANES)]
                total += dot(
                    jnp.concatenate([low, high], axis=1), pack_sel[side * phases + phase]
                )
            packed[n, side] = total.astype(BF16)
            for k in (3, 0, 5) if side == 0 else (4, 2, 7):
                there, copy = halo_copy(pad, n, k)
                pl.when(there)(copy.start)

    def halo_finish(pad, n):
        for k in range(8):
            there, copy = halo_copy(pad, n, k)
            _, back = halo_copy(pad, n, 7 - k)

            @pl.when(there)
            def _(copy=copy, back=back):
                back.wait_recv()
                copy.wait_send()

        for side, lane in ((0, 0), (1, width + LANES)):
            at = pl.ds(lane, LANES)

            def body(phase, carry, side=side, at=at):
                placed = dot(strips[n, side], unpack_sel[side * phases + phase]).astype(BF16)
                pad[phase, pl.ds(chans, fold_rows), at] = placed[:fold_rows, :LANES]
                pad[phase, pl.ds(chans + fold_rows, fold_rows), at] = placed[:fold_rows, LANES:]
                pad[phase, pl.ds(0, chans), at] = placed[fold_rows : fold_rows + chans, LANES:]
                pad[phase, pl.ds(full - chans, chans), at] = placed[fold_rows + chans :, :LANES]
                return carry

            lax.fori_loop(0, phases, body, 0, unroll=4)

    tiles = width // LANES

    def held(at):
        return jnp.concatenate([hidden[k, at, :] for k in range(tiles)], axis=1)

    def keep(at, values):
        for k in range(tiles):
            hidden[k, at, :] = values[:, k * LANES : (k + 1) * LANES]

    def fold(values):
        total = jnp.sum(values.reshape(-1, chans, width), axis=0)
        return sum(total[:, k : k + LANES] for k in range(0, width, LANES))

    def conv(pad, n):
        def body(phase, acc):
            shifted = [
                pad[phase, :, pl.ds(LANES + (b - 1) * STEP, width)] for b in range(3)
            ]
            for g in range(count // GROUP):
                low = g * GROUP * chans
                high = low + (GROUP + 2) * chans
                result = sum(dot(weights[n, b], shifted[b][low:high]) for b in range(3))
                keep(pl.ds(phase * depth + low, GROUP * chans), result)
                acc = acc + fold(result)
            return acc

        return lax.fori_loop(0, phases, body, jnp.zeros((chans, LANES), F32), unroll=2)

    square = (chans, LANES)
    diagonal = iota(square, 0) == iota(square, 1)

    def to_lanes(values):
        return jnp.sum(jnp.where(diagonal, values, 0.0), axis=0, keepdims=True)

    def to_rows(values):
        spread = jnp.where(diagonal, jnp.broadcast_to(values, square), 0.0)
        return jnp.broadcast_to(jnp.sum(spread, axis=1, keepdims=True), square)

    def merge(own, other, size, stats, sends, recvs, n, axis_size, along_row):
        base = n * axis_size
        stats[base, pl.ds(0, 1), :] = own
        stats[base, pl.ds(1, 1), :] = other
        copies = []
        for d in range(1, axis_size):
            device = (
                (lax.rem(row + d, axis_size), col)
                if along_row
                else (row, lax.rem(col + d, axis_size))
            )
            copy = remote(
                stats.at[base],
                stats.at[base + d],
                sends.at[base + d],
                recvs.at[base + d],
                device,
            )
            copy.start()
            copies.append(copy)
        for copy in copies:
            copy.wait()
        means = [stats[base + d, pl.ds(0, 1), :] for d in range(axis_size)]
        mean = sum(means) / axis_size
        squares = sum(stats[base + d, pl.ds(1, 1), :] for d in range(axis_size))
        spread = sum((m - mean) * (m - mean) for m in means)
        return mean, squares + size * spread

    def norm(acc, n, gain, shift):
        own = jnp.broadcast_to(jnp.sum(acc, axis=1, keepdims=True) / cells, square)
        across = jnp.concatenate([own] * (width // LANES), axis=1)

        def body(phase, squares):
            for q in range(count):
                at = pl.ds(phase * depth + q * chans, chans)
                diff = held(at) - across
                squares = squares + fold(diff * diff)
            return squares

        squares = lax.fori_loop(0, phases, body, jnp.zeros(square, F32))
        squares = jnp.broadcast_to(jnp.sum(squares, axis=1, keepdims=True), square)
        mean, squares = merge(
            to_lanes(own), to_lanes(squares), cells, col_stats, cs_send, cs_recv, n, cols, False
        )
        mean, squares = merge(
            mean, squares, cells * cols, row_stats, rs_send, rs_recv, n, rows, True
        )
        factor = gain[...] * lax.rsqrt(squares / (cells * (rows * cols)) + EPSILON)
        repeat = lambda v: jnp.concatenate([to_rows(v)] * (width // LANES), axis=1)
        return repeat(mean), repeat(factor), repeat(shift[...])

    halo_start(pad_one, 0)
    band(0, first_ref)
    band(1, second_ref)
    halo_finish(pad_one, 0)
    mean, factor, shift = norm(conv(pad_one, 0), 0, gain_one, shift_one)

    def activate(phase, carry):
        for q in range(count):
            cell = held(pl.ds(phase * depth + q * chans, chans))
            cell = jnp.maximum((cell - mean) * factor + shift, 0.0)
            pad_two[phase, pl.ds((q + 1) * chans, chans), centre] = cell.astype(BF16)
        return carry

    lax.fori_loop(0, phases, activate, 0)
    halo_start(pad_two, 1)
    halo_finish(pad_two, 1)
    mean, factor, shift = norm(conv(pad_two, 1), 1, gain_two, shift_two)

    def finish(phase, carry):
        for q in range(count):
            at = pl.ds(phase * depth + q * chans, chans)
            cell = (held(at) - mean) * factor + shift
            cell = (x_ref[phase, pl.ds(q * chans, chans), :].astype(F32) + cell).astype(BF16)
            summed[phase, q] = cell
            keep(at, cell.astype(F32))
        return carry

    lax.fori_loop(0, phases, finish, 0)

    def direct(source_col, source_block):
        z, p = lax.rem(source_col, 4), lax.rem(source_block, 4)
        chosen = (z == p) & (lax.rem(source_col + source_block, 8) < 4)
        for a, b in DIRECT:
            chosen = chosen | ((z == a) & (p == b))
        return chosen

    mine = direct(col, block)

    def band_of(k):
        return pl.ds((k // phases) * PART, PART)

    def source(h, k):
        return summed.at[k % phases, :, band_of(k), pl.ds(h * height, height)]

    def landing(e, k):
        return got.at[k % phases, pl.ds(e * count, count), band_of(k), :]

    def waypoint(slot, k):
        return relay.at[slot, k % phases, :, band_of(k), :]

    def straight(h, k):
        return remote(
            source(h, k),
            landing(part, k),
            send.at[h * pieces + k],
            recv.at[part * pieces + k],
            (ratio * col + h, block),
        )

    def arrive(e, k):
        return remote(
            landing(e, k),
            landing(e, k),
            send.at[e * pieces + k],
            recv.at[e * pieces + k],
            (row, col),
        )

    def first_leg(h, k):
        slot = (lax.rem(block - col + cols, cols) - 1) * ratio + part
        return remote(
            source(h, k),
            waypoint(slot, k),
            send.at[h * pieces + k],
            relay_recv.at[slot * pieces + k],
            (ratio * col + h, col),
        )

    def second_leg(d, e, k):
        slot = (d - 1) * ratio + e
        return remote(
            waypoint(slot, k),
            landing(e, k),
            relay_send.at[slot * pieces + k],
            recv.at[e * pieces + k],
            (row, lax.rem(col + d, cols)),
        )

    @pl.when(jnp.logical_not(relays) & mine)
    def _():
        for k in range(pieces):
            for h in range(ratio):
                straight(h, k).start()

    @pl.when(jnp.logical_not(relays | mine))
    def _():
        for k in range(pieces):
            for h in range(ratio):
                first_leg(h, k).start()

    @pl.when(relays)
    def _():
        for h in range(ratio):

            @pl.when(part != h)
            def _(h=h):
                for k in range(pieces):
                    straight(h, k).start()

            @pl.when(part == h)
            def _(h=h):
                got[:, pl.ds(h * count, count), :, :] = summed[
                    :, :, :, pl.ds(h * height, height)
                ]

        for k in range(pieces):
            for d in range(1, cols):

                @pl.when(jnp.logical_not(direct(col, lax.rem(col + d, cols))))
                def _(d=d, k=k):
                    for e in range(ratio):
                        slot = (d - 1) * ratio + e
                        remote(
                            waypoint(slot, k),
                            waypoint(slot, k),
                            relay_send.at[slot * pieces + k],
                            relay_recv.at[slot * pieces + k],
                            (row, col),
                        ).wait_recv()
                        second_leg(d, e, k).start()

    span = ratio * depth
    for p in range(parts):
        for phase in range(phases):
            k = p * phases + phase
            for e in range(ratio):

                @pl.when(jnp.logical_not(relays & (part == e)))
                def _(e=e, k=k):
                    arrive(e, k).wait_recv()

            def unfold(q, carry, p=p, phase=phase):
                wide[pl.ds(phase * span + q * chans + p * PART, PART), :] = got[
                    phase, q, pl.ds(p * PART, PART), :
                ].astype(F32)
                return carry

            lax.fori_loop(0, ratio * count, unfold, 0, unroll=8)

        def turn(c, carry):
            own = jnp.concatenate(
                [
                    held(pl.ds(q * chans + c, phases, stride=depth))
                    for q in range(count)
                ],
                axis=0,
            )
            other = jnp.concatenate(
                [
                    wide[pl.ds(q * chans + c, phases, stride=span), :]
                    for q in range(ratio * count)
                ],
                axis=0,
            )
            total = own + jnp.swapaxes(other, 0, 1)
            out_ref[c] = (total * 0.5).astype(BF16)
            return carry

        lax.fori_loop(p * PART, (p + 1) * PART, turn, 0)

    for k in range(pieces):
        for h in range(ratio):

            @pl.when(jnp.logical_not(relays & (part == h)))
            def _(h=h, k=k):
                straight(h, k).wait_send()

    @pl.when(relays)
    def _():
        for k in range(pieces):
            for d in range(1, cols):

                @pl.when(jnp.logical_not(direct(col, lax.rem(col + d, cols))))
                def _(d=d, k=k):
                    for e in range(ratio):
                        second_leg(d, e, k).wait_send()


def run(rows, cols, features, first, second, scales):
    chans, height, width = features.shape
    count = height // STEP
    depth = count * chans
    ratio = rows // cols
    slots = (cols - 1) * ratio
    pieces = (chans // PART) * STEP
    full = depth + 2 * chans
    x = jnp.transpose(features.reshape(chans, count, STEP, width), (2, 1, 0, 3))
    x = x.reshape(STEP, depth, width)
    scales = [jnp.pad(v, (0, LANES - chans)).reshape(1, LANES) for v in scales]
    vmem = pl.BlockSpec(memory_space=pltpu.VMEM)
    dma = pltpu.SemaphoreType.DMA
    return pl.pallas_call(
        functools.partial(kernel, rows, cols),
        out_shape=jax.ShapeDtypeStruct(features.shape, BF16),
        in_specs=[vmem] * 7,
        out_specs=vmem,
        scratch_shapes=[
            pltpu.VMEM((STEP, full, width + 2 * LANES), BF16),
            pltpu.VMEM((STEP, full, width + 2 * LANES), BF16),
            pltpu.VMEM((width // LANES, STEP * depth, LANES), F32),
            pltpu.VMEM((2 * STEP, 2 * LANES, LANES), BF16),
            pltpu.VMEM((2 * STEP, LANES, 2 * LANES), BF16),
            pltpu.VMEM((2, 3, GROUP * chans, (GROUP + 2) * chans), BF16),
            pltpu.VMEM((2, 2, depth // 2, LANES), BF16),
            pltpu.VMEM((2, 2, depth // 2 + 2 * chans, LANES), BF16),
            pltpu.VMEM((2 * cols, 8, LANES), F32),
            pltpu.VMEM((2 * rows, 8, LANES), F32),
            pltpu.VMEM((STEP, count, chans, width), BF16),
            pltpu.VMEM((STEP, ratio * count, chans, height), BF16),
            pltpu.VMEM((STEP * ratio * depth, height), F32),
            pltpu.VMEM((slots, STEP, count, chans, height), BF16),
            dma((16,)),
            dma((16,)),
            dma((2 * cols,)),
            dma((2 * cols,)),
            dma((2 * rows,)),
            dma((2 * rows,)),
            dma((ratio * pieces,)),
            dma((ratio * pieces,)),
            dma((slots * pieces,)),
            dma((slots * pieces,)),
        ],
        compiler_params=pltpu.CompilerParams(
            collective_id=0, has_side_effects=True, vmem_limit_bytes=56 * 1024 * 1024
        ),
    )(x, first, second, *scales)


def solution(mesh):
    rows, cols = mesh.shape["row"], mesh.shape["col"]

    def per_device(features, first, second, gain_one, shift_one, gain_two, shift_two):
        scales = (gain_one, shift_one, gain_two, shift_two)
        return run(rows, cols, features, first, second, scales)

    placed = (P(None, "row", "col"), P(), P(), P(), P(), P(), P())
    return jax.shard_map(
        per_device, mesh=mesh, in_specs=placed, out_specs=P(None, "row", "col"), check_vma=False
    )
```

```python
import functools

import jax
import jax.numpy as jnp
from jax import lax
from jax.experimental import pallas as pl
from jax.experimental.pallas import tpu as pltpu
from jax.sharding import PartitionSpec as P

STEP = 8
GROUP = 4
EPSILON = 1e-05
LANES = 128
PART = 16
MESH = pl.DeviceIdType.MESH
BF16 = jnp.bfloat16
F32 = jnp.float32

DIRECT = ((0, 1), (0, 2), (1, 3), (2, 0), (3, 1), (3, 2))

WAYS = ((-1, -1), (-1, 0), (-1, 1), (0, -1), (0, 1), (1, -1), (1, 0), (1, 1))


def iota(shape, dim):
    return lax.broadcasted_iota(jnp.int32, shape, dim)


def one_hot(mask):
    return jnp.where(mask, 1.0, 0.0).astype(BF16)


def dot(a, b):
    return jnp.dot(a, b, preferred_element_type=F32)


def remote(src, dst, send, recv, device):
    return pltpu.make_async_remote_copy(
        src_ref=src,
        dst_ref=dst,
        send_sem=send,
        recv_sem=recv,
        device_id=device,
        device_id_type=MESH,
    )


def kernel(
    rows,
    cols,
    x_ref,
    first_ref,
    second_ref,
    gain_one,
    shift_one,
    gain_two,
    shift_two,
    out_ref,
    pad_one,
    pad_two,
    hidden,
    pack_sel,
    weights,
    packed,
    strips,
    col_stats,
    row_stats,
    summed,
    got,
    wide,
    relay,
    halo_send,
    halo_recv,
    cs_send,
    cs_recv,
    rs_send,
    rs_recv,
    send,
    recv,
    relay_send,
    relay_recv,
):
    row = lax.axis_index("row")
    col = lax.axis_index("col")
    phases, depth, width = x_ref.shape
    chans, height, _ = out_ref.shape
    count = depth // chans
    full = depth + 2 * chans
    fold_rows = depth // 2
    half_lanes = LANES // 2
    cells = float(phases * count * width)
    centre = pl.ds(LANES, width)
    ratio = rows // cols
    block = lax.div(row, ratio)
    part = lax.rem(row, ratio)
    relays = block == col
    parts = chans // PART
    pieces = parts * phases

    for pad in (pad_one, pad_two):
        for at, size in ((0, chans), (depth + chans, chans)):
            pad[:, pl.ds(at, size), :] = jnp.zeros((phases, size, width + 2 * LANES), BF16)
        for at in (0, width + LANES):
            pad[:, pl.ds(chans, depth), pl.ds(at, LANES)] = jnp.zeros(
                (phases, depth, LANES), BF16
            )
    strips[...] = jnp.zeros_like(strips)

    barrier = pltpu.get_barrier_semaphore()

    def greet(device):
        pl.semaphore_signal(barrier, inc=1, device_id=device, device_id_type=MESH)

    def neighbour(k):
        dr, dc = WAYS[k]
        there = jnp.bool_(True)
        if dr:
            there = there & ((row > 0) if dr < 0 else (row < rows - 1))
        if dc:
            there = there & ((col > 0) if dc < 0 else (col < cols - 1))
        device = (jnp.clip(row + dr, 0, rows - 1), jnp.clip(col + dc, 0, cols - 1))
        return there, device

    expected = jnp.int32(rows + cols - 2)
    for d in range(1, cols):
        greet((row, lax.rem(col + d, cols)))
    for d in range(1, rows):
        greet((lax.rem(row + d, rows), col))
    for k in (0, 2, 5, 7):
        there, device = neighbour(k)
        pl.when(there)(functools.partial(greet, device))
        expected = expected + jnp.where(there, 1, 0)
    for h in range(ratio):
        pl.when(jnp.logical_not(relays))(functools.partial(greet, (ratio * col + h, block)))
    expected = expected + jnp.where(relays, 0, ratio)

    pad_one[:, pl.ds(chans, depth), centre] = x_ref[...]

    i, j = iota((2 * LANES, LANES), 0), iota((2 * LANES, LANES), 1)
    edge = LANES - STEP
    lane = i % LANES
    goal = (i // LANES) * half_lanes + lane - j
    head = jnp.where(lane < STEP, goal, -LANES)
    tail = jnp.where(lane >= edge, goal - edge, -LANES)
    for phase in range(phases):
        pack_sel[phase] = one_hot(head == -phase * STEP)
        pack_sel[phases + phase] = one_hot(tail == -phase * STEP)

    def band(n, kernel_ref):
        span = (GROUP + 2) * chans
        c, k = iota((chans, span), 0), iota((chans, span), 1)
        for q in range(GROUP):
            for b in range(3):
                total = jnp.zeros((chans, span), F32)
                for a in range(3):
                    total += dot(kernel_ref[a, b], one_hot(k == c + (q + a) * chans))
                weights[n, b, pl.ds(q * chans, chans), :] = total.astype(BF16)

    pl.semaphore_wait(barrier, expected)

    def halo_copy(pad, n, k):
        dr, dc = WAYS[k]
        there, device = neighbour(k)
        if dc == 0:
            source = chans if dr < 0 else depth
            target = depth + chans if dr < 0 else 0
            src = pad.at[:, pl.ds(source, chans), centre]
            dst = pad.at[:, pl.ds(target, chans), centre]
        else:
            mine, theirs = (0, 1) if dc < 0 else (1, 0)
            if dr == 0:
                src = packed.at[n, mine]
                dst = strips.at[n, theirs, pl.ds(0, fold_rows)]
            elif dr < 0:
                src = packed.at[n, mine, pl.ds(0, chans)]
                dst = strips.at[n, theirs, pl.ds(fold_rows + chans, chans)]
            else:
                src = packed.at[n, mine, pl.ds(fold_rows - chans, chans)]
                dst = strips.at[n, theirs, pl.ds(fold_rows, chans)]
        slot = n * 8 + k
        return there, remote(src, dst, halo_send.at[slot], halo_recv.at[slot], device)

    def halo_start(pad, n):
        for k in (1, 6):
            there, copy = halo_copy(pad, n, k)
            pl.when(there)(copy.start)
        for side, lane in ((0, LANES), (1, width)):
            total = jnp.zeros((fold_rows, LANES), F32)
            for phase in range(phases):
                low = pad[phase, pl.ds(chans, fold_rows), pl.ds(lane, LANES)]
                high = pad[phase, pl.ds(chans + fold_rows, fold_rows), pl.ds(lane, LANES)]
                total += dot(
                    jnp.concatenate([low, high], axis=1), pack_sel[side * phases + phase]
                )
            packed[n, side] = total.astype(BF16)
            for k in (3, 0, 5) if side == 0 else (4, 2, 7):
                there, copy = halo_copy(pad, n, k)
                pl.when(there)(copy.start)

    def halo_finish(pad, n):
        for k in range(8):
            there, copy = halo_copy(pad, n, k)
            _, back = halo_copy(pad, n, 7 - k)

            @pl.when(there)
            def _(copy=copy, back=back):
                back.wait_recv()
                copy.wait_send()

    tiles = width // LANES

    def held(at):
        return jnp.concatenate([hidden[k, at, :] for k in range(tiles)], axis=1)

    def keep(at, values):
        for k in range(tiles):
            hidden[k, at, :] = values[:, k * LANES : (k + 1) * LANES]

    def fold(values):
        total = jnp.sum(values.reshape(-1, chans, width), axis=0)
        return sum(total[:, k : k + LANES] for k in range(0, width, LANES))

    def taps(pad, n, groups, acc):
        def body(phase, acc):
            for first, last in groups:
                low = first * GROUP * chans
                rows_in = ((last - first) * GROUP + 2) * chans
                shifted = [
                    pad[phase, pl.ds(low, rows_in), pl.ds(LANES + (b - 1) * STEP, width)]
                    for b in range(3)
                ]
                for g in range(last - first):
                    at = g * GROUP * chans
                    result = sum(
                        dot(weights[n, b], shifted[b][at : at + (GROUP + 2) * chans])
                        for b in range(3)
                    )
                    keep(pl.ds(phase * depth + low + at, GROUP * chans), result)
                    acc = acc + fold(result)
            return acc

        return lax.fori_loop(0, phases, body, acc, unroll=2)

    def strip_taps(n, side, acc):
        swap = lambda v: jnp.concatenate([v[:, half_lanes:], v[:, :half_lanes]], axis=1)
        whole = strips[n, side, pl.ds(0, fold_rows), :]
        up = strips[n, side, pl.ds(fold_rows, chans), :]
        down = strips[n, side, pl.ds(fold_rows + chans, chans), :]
        column = jnp.concatenate([swap(up), whole, swap(whole), down], axis=0)
        lanes = iota((GROUP * chans, LANES), 1)
        if side == 0:
            tile, start, wanted = 0, 0, lanes < STEP
        else:
            tile, start, wanted = tiles - 1, edge, lanes >= edge
        for g in range(count // GROUP):
            low = g * GROUP * chans
            added = dot(weights[n, 2 * side], column[low : low + (GROUP + 2) * chans])
            added = jnp.where(lanes < half_lanes, added, 0.0)
            acc = acc + jnp.sum(added.reshape(GROUP, chans, LANES), axis=0)
            for phase in range(phases):
                at = pl.ds(phase * depth + low, GROUP * chans)
                moved = pltpu.roll(added, (start - phase * STEP) % LANES, 1)
                hidden[tile, at, :] = hidden[tile, at, :] + jnp.where(wanted, moved, 0.0)
        return acc

    def conv(pad, n):
        last = count // GROUP
        acc = taps(pad, n, ((1, last - 1),), jnp.zeros((chans, LANES), F32))
        halo_finish(pad, n)
        acc = taps(pad, n, ((0, 1), (last - 1, last)), acc)
        for side in range(2):
            acc = strip_taps(n, side, acc)
        return acc

    square = (chans, LANES)
    diagonal = iota(square, 0) == iota(square, 1)

    def to_lanes(values):
        return jnp.sum(jnp.where(diagonal, values, 0.0), axis=0, keepdims=True)

    def to_rows(values):
        spread = jnp.where(diagonal, jnp.broadcast_to(values, square), 0.0)
        return jnp.broadcast_to(jnp.sum(spread, axis=1, keepdims=True), square)

    def merge(own, other, size, stats, sends, recvs, n, axis_size, along_row):
        base = n * axis_size
        stats[base, pl.ds(0, 1), :] = own
        stats[base, pl.ds(1, 1), :] = other
        copies = []
        for d in range(1, axis_size):
            device = (
                (lax.rem(row + d, axis_size), col)
                if along_row
                else (row, lax.rem(col + d, axis_size))
            )
            copy = remote(
                stats.at[base],
                stats.at[base + d],
                sends.at[base + d],
                recvs.at[base + d],
                device,
            )
            copy.start()
            copies.append(copy)
        for copy in copies:
            copy.wait()
        means = [stats[base + d, pl.ds(0, 1), :] for d in range(axis_size)]
        mean = sum(means) / axis_size
        squares = sum(stats[base + d, pl.ds(1, 1), :] for d in range(axis_size))
        spread = sum((m - mean) * (m - mean) for m in means)
        return mean, squares + size * spread

    def norm(acc, n, gain, shift):
        own = jnp.broadcast_to(jnp.sum(acc, axis=1, keepdims=True) / cells, square)
        across = jnp.concatenate([own] * (width // LANES), axis=1)

        def body(phase, squares):
            for q in range(count):
                at = pl.ds(phase * depth + q * chans, chans)
                diff = held(at) - across
                squares = squares + fold(diff * diff)
            return squares

        squares = lax.fori_loop(0, phases, body, jnp.zeros(square, F32), unroll=2)
        squares = jnp.broadcast_to(jnp.sum(squares, axis=1, keepdims=True), square)
        mean, squares = merge(
            to_lanes(own), to_lanes(squares), cells, col_stats, cs_send, cs_recv, n, cols, False
        )
        mean, squares = merge(
            mean, squares, cells * cols, row_stats, rs_send, rs_recv, n, rows, True
        )
        blank = jnp.zeros((1, LANES - chans), F32)
        gains = jnp.concatenate([gain[...], blank], axis=1)
        shifts = jnp.concatenate([shift[...], blank], axis=1)
        factor = gains * lax.rsqrt(squares / (cells * (rows * cols)) + EPSILON)
        repeat = lambda v: jnp.concatenate([to_rows(v)] * (width // LANES), axis=1)
        return repeat(mean), repeat(factor), repeat(shifts)

    halo_start(pad_one, 0)
    band(0, first_ref)
    band(1, second_ref)
    mean, factor, shift = norm(conv(pad_one, 0), 0, gain_one, shift_one)

    def activate(phase, carry):
        for q in range(count):
            cell = held(pl.ds(phase * depth + q * chans, chans))
            cell = jnp.maximum((cell - mean) * factor + shift, 0.0)
            pad_two[phase, pl.ds((q + 1) * chans, chans), centre] = cell.astype(BF16)
        return carry

    lax.fori_loop(0, phases, activate, 0)
    halo_start(pad_two, 1)
    mean, factor, shift = norm(conv(pad_two, 1), 1, gain_two, shift_two)

    def direct(source_col, source_block):
        z, p = lax.rem(source_col, 4), lax.rem(source_block, 4)
        chosen = (z == p) & (lax.rem(source_col + source_block, 8) < 4)
        for a, b in DIRECT:
            chosen = chosen | ((z == a) & (p == b))
        return chosen

    mine = direct(col, block)

    def band_of(k):
        return pl.ds(pl.multiple_of((k // phases) * PART, PART), PART)

    def source(h, k):
        return summed.at[k % phases, :, band_of(k), pl.ds(h * height, height)]

    def landing(e, k):
        return got.at[k % phases, pl.ds(e * count, count), band_of(k), :]

    def waypoint(slot, k):
        return relay.at[slot, k % phases, :, band_of(k), :]

    def straight(h, k):
        return remote(
            source(h, k),
            landing(part, k),
            send.at[h * pieces + k],
            recv.at[part * pieces + k],
            (ratio * col + h, block),
        )

    def arrive(e, k):
        return remote(
            landing(e, k),
            landing(e, k),
            send.at[e * pieces + k],
            recv.at[e * pieces + k],
            (row, col),
        )

    def first_leg(h, k):
        slot = (lax.rem(block - col + cols, cols) - 1) * ratio + part
        return remote(
            source(h, k),
            waypoint(slot, k),
            send.at[h * pieces + k],
            relay_recv.at[slot * pieces + k],
            (ratio * col + h, col),
        )

    def second_leg(d, e, k):
        slot = (d - 1) * ratio + e
        return remote(
            waypoint(slot, k),
            landing(e, k),
            relay_send.at[slot * pieces + k],
            recv.at[e * pieces + k],
            (row, lax.rem(col + d, cols)),
        )

    def issue(k):
        goes = relays | mine | (k == pieces - 1)
        for h in range(ratio):
            here = relays & (part == h)

            @pl.when(goes & jnp.logical_not(here))
            def _(h=h):
                straight(h, k).start()

            @pl.when(jnp.logical_not(goes))
            def _(h=h):
                first_leg(h, k).start()

    def finish(phase, carry):
        for q in range(count):
            at = pl.ds(phase * depth + q * chans, chans)
            cell = (held(at) - mean) * factor + shift
            cell = (x_ref[phase, pl.ds(q * chans, chans), :].astype(F32) + cell).astype(BF16)
            summed[phase, q] = cell
            keep(at, cell.astype(F32))
        issue(phase)
        return carry

    lax.fori_loop(0, phases, finish, 0)

    def issue_rest(k, carry):
        issue(k)
        return carry

    lax.fori_loop(phases, pieces, issue_rest, 0)

    @pl.when(relays)
    def _():
        for h in range(ratio):

            @pl.when(part == h)
            def _(h=h):
                got[:, pl.ds(h * count, count), :, :] = summed[
                    :, :, :, pl.ds(h * height, height)
                ]

        def forward(k, carry):
            for d in range(1, cols):

                @pl.when(jnp.logical_not(direct(col, lax.rem(col + d, cols))))
                def _(d=d):
                    for e in range(ratio):
                        slot = (d - 1) * ratio + e
                        remote(
                            waypoint(slot, k),
                            waypoint(slot, k),
                            relay_send.at[slot * pieces + k],
                            relay_recv.at[slot * pieces + k],
                            (row, col),
                        ).wait_recv()
                        second_leg(d, e, k).start()

            return carry

        lax.fori_loop(0, pieces - 1, forward, 0)

    span = ratio * depth
    for p in range(parts):
        def collect(phase, carry, p=p):
            k = p * phases + phase
            for e in range(ratio):

                @pl.when(jnp.logical_not(relays & (part == e)))
                def _(e=e):
                    arrive(e, k).wait_recv()

            for q in range(ratio * count):
                wide[pl.ds(phase * span + q * chans + p * PART, PART), :] = got[
                    phase, q, pl.ds(p * PART, PART), :
                ].astype(F32)
            return carry

        lax.fori_loop(0, phases, collect, 0)

        def turn(c, carry):
            own = jnp.concatenate(
                [
                    held(pl.ds(q * chans + c, phases, stride=depth))
                    for q in range(count)
                ],
                axis=0,
            )
            other = jnp.concatenate(
                [
                    wide[pl.ds(q * chans + c, phases, stride=span), :]
                    for q in range(ratio * count)
                ],
                axis=0,
            )
            total = own + jnp.swapaxes(other, 0, 1)
            out_ref[c] = (total * 0.5).astype(BF16)
            return carry

        lax.fori_loop(p * PART, (p + 1) * PART, turn, 0, unroll=4)

    def drain(k, carry):
        for h in range(ratio):

            @pl.when(jnp.logical_not(relays & (part == h)))
            def _(h=h):
                straight(h, k).wait_send()

        return carry

    lax.fori_loop(0, pieces, drain, 0)

    @pl.when(relays)
    def _():
        def drain_relay(k, carry):
            for d in range(1, cols):

                @pl.when(jnp.logical_not(direct(col, lax.rem(col + d, cols))))
                def _(d=d):
                    for e in range(ratio):
                        second_leg(d, e, k).wait_send()

            return carry

        lax.fori_loop(0, pieces - 1, drain_relay, 0)


def run(rows, cols, features, first, second, scales):
    chans, height, width = features.shape
    count = height // STEP
    depth = count * chans
    ratio = rows // cols
    slots = (cols - 1) * ratio
    pieces = (chans // PART) * STEP
    full = depth + 2 * chans
    x = jnp.transpose(features.reshape(chans, count, STEP, width), (2, 1, 0, 3))
    x = x.reshape(STEP, depth, width)
    scales = [v.reshape(1, chans) for v in scales]
    vmem = pl.BlockSpec(memory_space=pltpu.VMEM)
    dma = pltpu.SemaphoreType.DMA
    return pl.pallas_call(
        functools.partial(kernel, rows, cols),
        out_shape=jax.ShapeDtypeStruct(features.shape, BF16),
        in_specs=[vmem] * 7,
        out_specs=vmem,
        scratch_shapes=[
            pltpu.VMEM((STEP, full, width + 2 * LANES), BF16),
            pltpu.VMEM((STEP, full, width + 2 * LANES), BF16),
            pltpu.VMEM((width // LANES, STEP * depth, LANES), F32),
            pltpu.VMEM((2 * STEP, 2 * LANES, LANES), BF16),
            pltpu.VMEM((2, 3, GROUP * chans, (GROUP + 2) * chans), BF16),
            pltpu.VMEM((2, 2, depth // 2, LANES), BF16),
            pltpu.VMEM((2, 2, depth // 2 + 2 * chans, LANES), BF16),
            pltpu.VMEM((2 * cols, 8, LANES), F32),
            pltpu.VMEM((2 * rows, 8, LANES), F32),
            pltpu.VMEM((STEP, count, chans, width), BF16),
            pltpu.VMEM((STEP, ratio * count, chans, height), BF16),
            pltpu.VMEM((STEP * ratio * depth, height), F32),
            pltpu.VMEM((slots, STEP, count, chans, height), BF16),
            dma((16,)),
            dma((16,)),
            dma((2 * cols,)),
            dma((2 * cols,)),
            dma((2 * rows,)),
            dma((2 * rows,)),
            dma((ratio * pieces,)),
            dma((ratio * pieces,)),
            dma((slots * pieces,)),
            dma((slots * pieces,)),
        ],
        compiler_params=pltpu.CompilerParams(
            collective_id=0, has_side_effects=True, vmem_limit_bytes=44 * 1024 * 1024
        ),
    )(x, first, second, *scales)


def solution(mesh):
    rows, cols = mesh.shape["row"], mesh.shape["col"]

    def per_device(features, first, second, gain_one, shift_one, gain_two, shift_two):
        scales = (gain_one, shift_one, gain_two, shift_two)
        return run(rows, cols, features, first, second, scales)

    placed = (P(None, "row", "col"), P(), P(), P(), P(), P(), P())
    return jax.shard_map(
        per_device, mesh=mesh, in_specs=placed, out_specs=P(None, "row", "col"), check_vma=False
    )
```

```python
import functools

import jax
import jax.numpy as jnp
from jax import lax
from jax.experimental import pallas as pl
from jax.experimental.pallas import tpu as pltpu
from jax.sharding import PartitionSpec as P

STEP = 8
GROUP = 4
EPSILON = 1e-05
LANES = 128
PART = 16
MESH = pl.DeviceIdType.MESH
BF16 = jnp.bfloat16
F32 = jnp.float32

DIRECT = ((0, 1), (0, 2), (1, 3), (2, 0), (3, 1), (3, 2))

WAYS = ((-1, -1), (-1, 0), (-1, 1), (0, -1), (0, 1), (1, -1), (1, 0), (1, 1))


def iota(shape, dim):
    return lax.broadcasted_iota(jnp.int32, shape, dim)


def one_hot(mask):
    return jnp.where(mask, 1.0, 0.0).astype(BF16)


def dot(a, b):
    return jnp.dot(a, b, preferred_element_type=F32)


def remote(src, dst, send, recv, device):
    return pltpu.make_async_remote_copy(
        src_ref=src,
        dst_ref=dst,
        send_sem=send,
        recv_sem=recv,
        device_id=device,
        device_id_type=MESH,
    )


def kernel(
    rows,
    cols,
    x_ref,
    first_ref,
    second_ref,
    gain_one,
    shift_one,
    gain_two,
    shift_two,
    out_ref,
    pad_one,
    pad_two,
    hidden,
    pack_sel,
    edges,
    weights,
    packed,
    strips,
    col_stats,
    row_stats,
    summed,
    got,
    wide,
    relay,
    halo_send,
    halo_recv,
    cs_send,
    cs_recv,
    rs_send,
    rs_recv,
    send,
    recv,
    relay_send,
    relay_recv,
):
    row = lax.axis_index("row")
    col = lax.axis_index("col")
    phases, depth, width = x_ref.shape
    chans, height, _ = out_ref.shape
    count = depth // chans
    full = depth + 2 * chans
    fold_rows = depth // 2
    half_lanes = LANES // 2
    cells = float(phases * count * width)
    ratio = rows // cols
    block = lax.div(row, ratio)
    part = lax.rem(row, ratio)
    relays = block == col
    parts = chans // PART
    pieces = parts * phases

    for pad in (pad_one, pad_two):
        for at, size in ((0, chans), (depth + chans, chans)):
            pad[:, pl.ds(at, size), :] = jnp.zeros((phases, size, width), BF16)
    strips[...] = jnp.zeros_like(strips)

    barrier = pltpu.get_barrier_semaphore()

    def greet(device):
        pl.semaphore_signal(barrier, inc=1, device_id=device, device_id_type=MESH)

    def neighbour(k):
        dr, dc = WAYS[k]
        there = jnp.bool_(True)
        if dr:
            there = there & ((row > 0) if dr < 0 else (row < rows - 1))
        if dc:
            there = there & ((col > 0) if dc < 0 else (col < cols - 1))
        device = (jnp.clip(row + dr, 0, rows - 1), jnp.clip(col + dc, 0, cols - 1))
        return there, device

    expected = jnp.int32(rows + cols - 2)
    for d in range(1, cols):
        greet((row, lax.rem(col + d, cols)))
    for d in range(1, rows):
        greet((lax.rem(row + d, rows), col))
    for k in (0, 2, 5, 7):
        there, device = neighbour(k)
        pl.when(there)(functools.partial(greet, device))
        expected = expected + jnp.where(there, 1, 0)
    for h in range(ratio):
        pl.when(jnp.logical_not(relays))(functools.partial(greet, (ratio * col + h, block)))
    expected = expected + jnp.where(relays, 0, ratio)

    pad_one[:, pl.ds(chans, depth), :] = x_ref[...]

    i, j = iota((2 * LANES, LANES), 0), iota((2 * LANES, LANES), 1)
    edge = LANES - STEP
    lane = i % LANES
    goal = (i // LANES) * half_lanes + lane - j
    head = jnp.where(lane < STEP, goal, -LANES)
    tail = jnp.where(lane >= edge, goal - edge, -LANES)
    for phase in range(phases):
        pack_sel[phase] = one_hot(head == -phase * STEP)
        pack_sel[phases + phase] = one_hot(tail == -phase * STEP)

    def band(n, kernel_ref):
        span = (GROUP + 2) * chans
        c, k = iota((chans, span), 0), iota((chans, span), 1)
        for q in range(GROUP):
            for b in range(3):
                total = jnp.zeros((chans, span), F32)
                for a in range(3):
                    total += dot(kernel_ref[a, b], one_hot(k == c + (q + a) * chans))
                weights[n, b, pl.ds(q * chans, chans), :] = total.astype(BF16)

    pl.semaphore_wait(barrier, expected)

    def halo_copy(pad, n, k):
        dr, dc = WAYS[k]
        there, device = neighbour(k)
        if dc == 0:
            source = chans if dr < 0 else depth
            target = depth + chans if dr < 0 else 0
            src = pad.at[:, pl.ds(source, chans)]
            dst = pad.at[:, pl.ds(target, chans)]
        else:
            mine, theirs = (0, 1) if dc < 0 else (1, 0)
            if dr == 0:
                src = packed.at[n, mine]
                dst = strips.at[n, theirs, pl.ds(0, fold_rows)]
            elif dr < 0:
                src = packed.at[n, mine, pl.ds(0, chans)]
                dst = strips.at[n, theirs, pl.ds(fold_rows + chans, chans)]
            else:
                src = packed.at[n, mine, pl.ds(fold_rows - chans, chans)]
                dst = strips.at[n, theirs, pl.ds(fold_rows, chans)]
        slot = n * 8 + k
        return there, remote(src, dst, halo_send.at[slot], halo_recv.at[slot], device)

    def halo_start(pad, n):
        for k in (1, 6):
            there, copy = halo_copy(pad, n, k)
            pl.when(there)(copy.start)
        for side, lane in ((0, 0), (1, width - LANES)):
            total = jnp.zeros((fold_rows, LANES), F32)
            for phase in range(phases):
                low = pad[phase, pl.ds(chans, fold_rows), pl.ds(lane, LANES)]
                high = pad[phase, pl.ds(chans + fold_rows, fold_rows), pl.ds(lane, LANES)]
                total += dot(
                    jnp.concatenate([low, high], axis=1), pack_sel[side * phases + phase]
                )
            packed[n, side] = total.astype(BF16)
            for k in (3, 0, 5) if side == 0 else (4, 2, 7):
                there, copy = halo_copy(pad, n, k)
                pl.when(there)(copy.start)

    def halo_finish(pad, n):
        for k in range(8):
            there, copy = halo_copy(pad, n, k)
            _, back = halo_copy(pad, n, 7 - k)

            @pl.when(there)
            def _(copy=copy, back=back):
                back.wait_recv()
                copy.wait_send()

    tiles = width // LANES

    def held(at):
        return jnp.concatenate([hidden[k, at, :] for k in range(tiles)], axis=1)

    def keep(at, values):
        for k in range(tiles):
            hidden[k, at, :] = values[:, k * LANES : (k + 1) * LANES]

    def fold(values):
        total = jnp.sum(values.reshape(-1, chans, width), axis=0)
        return sum(total[:, k : k + LANES] for k in range(0, width, LANES))

    def taps(pad, n, groups, acc):
        def body(phase, acc):
            for first, last in groups:
                low = first * GROUP * chans
                rows_in = ((last - first) * GROUP + 2) * chans
                middle = pad[phase, pl.ds(low, rows_in), :]
                blank = jnp.zeros((rows_in, STEP), BF16)
                shifted = (
                    jnp.concatenate([blank, middle[:, : width - STEP]], axis=1),
                    middle,
                    jnp.concatenate([middle[:, STEP:], blank], axis=1),
                )
                for g in range(last - first):
                    at = g * GROUP * chans
                    result = sum(
                        dot(weights[n, b], shifted[b][at : at + (GROUP + 2) * chans])
                        for b in range(3)
                    )
                    keep(pl.ds(phase * depth + low + at, GROUP * chans), result)
                    acc = acc + fold(result)
            return acc

        return lax.fori_loop(0, phases, body, acc, unroll=True)

    lanes = iota((GROUP * chans, LANES), 1)

    def strip_taps(n, side, acc):
        swap = lambda v: jnp.concatenate([v[:, half_lanes:], v[:, :half_lanes]], axis=1)
        whole = strips[n, side, pl.ds(0, fold_rows), :]
        up = strips[n, side, pl.ds(fold_rows, chans), :]
        down = strips[n, side, pl.ds(fold_rows + chans, chans), :]
        column = jnp.concatenate([swap(up), whole, swap(whole), down], axis=0)
        for g in range(count // GROUP):
            low = g * GROUP * chans
            added = dot(weights[n, 2 * side], column[low : low + (GROUP + 2) * chans])
            added = jnp.where(lanes < half_lanes, added, 0.0)
            edges[side, pl.ds(low, GROUP * chans), :] = added
            acc = acc + jnp.sum(added.reshape(GROUP, chans, LANES), axis=0)
        return acc

    def conv(pad, n):
        last = count // GROUP
        acc = taps(pad, n, ((1, last - 1),), jnp.zeros((chans, LANES), F32))
        halo_finish(pad, n)
        acc = taps(pad, n, ((0, 1), (last - 1, last)), acc)
        for side in range(2):
            acc = strip_taps(n, side, acc)
        return acc

    square = (chans, LANES)
    diagonal = iota(square, 0) == iota(square, 1)

    def to_lanes(values):
        return jnp.sum(jnp.where(diagonal, values, 0.0), axis=0, keepdims=True)

    def to_rows(values):
        spread = jnp.where(diagonal, jnp.broadcast_to(values, square), 0.0)
        return jnp.broadcast_to(jnp.sum(spread, axis=1, keepdims=True), square)

    def merge(own, other, size, stats, sends, recvs, n, axis_size, along_row):
        base = n * axis_size
        stats[base, pl.ds(0, 1), :] = own
        stats[base, pl.ds(1, 1), :] = other
        copies = []
        for d in range(1, axis_size):
            device = (
                (lax.rem(row + d, axis_size), col)
                if along_row
                else (row, lax.rem(col + d, axis_size))
            )
            copy = remote(
                stats.at[base],
                stats.at[base + d],
                sends.at[base + d],
                recvs.at[base + d],
                device,
            )
            copy.start()
            copies.append(copy)
        for copy in copies:
            copy.wait()
        means = [stats[base + d, pl.ds(0, 1), :] for d in range(axis_size)]
        mean = sum(means) / axis_size
        squares = sum(stats[base + d, pl.ds(1, 1), :] for d in range(axis_size))
        spread = sum((m - mean) * (m - mean) for m in means)
        return mean, squares + size * spread

    def norm(acc, n, gain, shift):
        own = jnp.broadcast_to(jnp.sum(acc, axis=1, keepdims=True) / cells, square)
        across = jnp.concatenate([own] * GROUP, axis=0)
        squares = jnp.zeros(square, F32)
        for phase in range(phases):
            for g in range(count // GROUP):
                low = g * GROUP * chans
                at = pl.ds(phase * depth + low, GROUP * chans)
                for k in range(tiles):
                    cell = hidden[k, at, :]
                    for side, tile, start in ((0, 0, 0), (1, tiles - 1, edge)):
                        if k == tile:
                            moved = pltpu.roll(
                                edges[side, pl.ds(low, GROUP * chans), :],
                                (start - phase * STEP) % LANES,
                                1,
                            )
                            wanted = lanes >= edge if side else lanes < STEP
                            cell = cell + jnp.where(wanted, moved, 0.0)
                            hidden[k, at, :] = cell
                    diff = cell - across
                    diff = (diff * diff).reshape(GROUP, chans, LANES)
                    squares = squares + jnp.sum(diff, axis=0)
        squares = jnp.broadcast_to(jnp.sum(squares, axis=1, keepdims=True), square)
        mean, squares = merge(
            to_lanes(own), to_lanes(squares), cells, col_stats, cs_send, cs_recv, n, cols, False
        )
        mean, squares = merge(
            mean, squares, cells * cols, row_stats, rs_send, rs_recv, n, rows, True
        )
        blank = jnp.zeros((1, LANES - chans), F32)
        gains = jnp.concatenate([gain[...], blank], axis=1)
        shifts = jnp.concatenate([shift[...], blank], axis=1)
        factor = gains * lax.rsqrt(squares / (cells * (rows * cols)) + EPSILON)
        repeat = lambda v: jnp.concatenate([to_rows(v)] * (width // LANES), axis=1)
        return repeat(mean), repeat(factor), repeat(shifts)

    halo_start(pad_one, 0)
    band(0, first_ref)
    band(1, second_ref)
    mean, factor, shift = norm(conv(pad_one, 0), 0, gain_one, shift_one)

    def activate(phase, carry):
        for q in range(count):
            cell = held(pl.ds(phase * depth + q * chans, chans))
            cell = jnp.maximum((cell - mean) * factor + shift, 0.0)
            pad_two[phase, pl.ds((q + 1) * chans, chans), :] = cell.astype(BF16)
        return carry

    lax.fori_loop(0, phases, activate, 0)
    halo_start(pad_two, 1)
    mean, factor, shift = norm(conv(pad_two, 1), 1, gain_two, shift_two)

    def direct(source_col, source_block):
        z, p = lax.rem(source_col, 4), lax.rem(source_block, 4)
        chosen = (z == p) & (lax.rem(source_col + source_block, 8) < 4)
        for a, b in DIRECT:
            chosen = chosen | ((z == a) & (p == b))
        return chosen

    mine = direct(col, block)

    def band_of(k):
        return pl.ds(pl.multiple_of((k // phases) * PART, PART), PART)

    def source(h, k):
        return summed.at[k % phases, :, band_of(k), pl.ds(h * height, height)]

    def landing(e, k):
        return got.at[k % phases, pl.ds(e * count, count), band_of(k), :]

    def waypoint(slot, k):
        return relay.at[slot, k % phases, :, band_of(k), :]

    def straight(h, k):
        return remote(
            source(h, k),
            landing(part, k),
            send.at[h * pieces + k],
            recv.at[part * pieces + k],
            (ratio * col + h, block),
        )

    def arrive(e, k):
        return remote(
            landing(e, k),
            landing(e, k),
            send.at[e * pieces + k],
            recv.at[e * pieces + k],
            (row, col),
        )

    def first_leg(h, k):
        slot = (lax.rem(block - col + cols, cols) - 1) * ratio + part
        return remote(
            source(h, k),
            waypoint(slot, k),
            send.at[h * pieces + k],
            relay_recv.at[slot * pieces + k],
            (ratio * col + h, col),
        )

    def second_leg(d, e, k):
        slot = (d - 1) * ratio + e
        return remote(
            waypoint(slot, k),
            landing(e, k),
            relay_send.at[slot * pieces + k],
            recv.at[e * pieces + k],
            (row, lax.rem(col + d, cols)),
        )

    def issue(k):
        goes = relays | mine | (k == pieces - 1)
        for h in range(ratio):
            here = relays & (part == h)

            @pl.when(goes & jnp.logical_not(here))
            def _(h=h):
                straight(h, k).start()

            @pl.when(jnp.logical_not(goes))
            def _(h=h):
                first_leg(h, k).start()

    def finish(phase, carry):
        for q in range(count):
            at = pl.ds(phase * depth + q * chans, chans)
            cell = (held(at) - mean) * factor + shift
            cell = (x_ref[phase, pl.ds(q * chans, chans), :].astype(F32) + cell).astype(BF16)
            summed[phase, q] = cell
            keep(at, cell.astype(F32))
        issue(phase)
        return carry

    lax.fori_loop(0, phases, finish, 0)

    def issue_rest(k, carry):
        issue(k)
        return carry

    lax.fori_loop(phases, pieces, issue_rest, 0)

    @pl.when(relays)
    def _():
        for h in range(ratio):

            @pl.when(part == h)
            def _(h=h):
                got[:, pl.ds(h * count, count), :, :] = summed[
                    :, :, :, pl.ds(h * height, height)
                ]

        def forward(k, carry):
            for d in range(1, cols):

                @pl.when(jnp.logical_not(direct(col, lax.rem(col + d, cols))))
                def _(d=d):
                    for e in range(ratio):
                        slot = (d - 1) * ratio + e
                        remote(
                            waypoint(slot, k),
                            waypoint(slot, k),
                            relay_send.at[slot * pieces + k],
                            relay_recv.at[slot * pieces + k],
                            (row, col),
                        ).wait_recv()
                        second_leg(d, e, k).start()

            return carry

        lax.fori_loop(0, pieces - 1, forward, 0)

    span = ratio * depth
    for p in range(parts):
        def collect(phase, carry, p=p):
            k = p * phases + phase
            for e in range(ratio):

                @pl.when(jnp.logical_not(relays & (part == e)))
                def _(e=e):
                    arrive(e, k).wait_recv()

            for q in range(ratio * count):
                wide[pl.ds(phase * span + q * chans + p * PART, PART), :] = got[
                    phase, q, pl.ds(p * PART, PART), :
                ].astype(F32)
            return carry

        lax.fori_loop(0, phases, collect, 0)

        def turn(c, carry):
            own = jnp.concatenate(
                [
                    held(pl.ds(q * chans + c, phases, stride=depth))
                    for q in range(count)
                ],
                axis=0,
            )
            other = jnp.concatenate(
                [
                    wide[pl.ds(q * chans + c, phases, stride=span), :]
                    for q in range(ratio * count)
                ],
                axis=0,
            )
            total = own + jnp.swapaxes(other, 0, 1)
            out_ref[c] = (total * 0.5).astype(BF16)
            return carry

        lax.fori_loop(p * PART, (p + 1) * PART, turn, 0, unroll=4)

    def drain(k, carry):
        for h in range(ratio):

            @pl.when(jnp.logical_not(relays & (part == h)))
            def _(h=h):
                straight(h, k).wait_send()

        return carry

    lax.fori_loop(0, pieces, drain, 0)

    @pl.when(relays)
    def _():
        def drain_relay(k, carry):
            for d in range(1, cols):

                @pl.when(jnp.logical_not(direct(col, lax.rem(col + d, cols))))
                def _(d=d):
                    for e in range(ratio):
                        second_leg(d, e, k).wait_send()

            return carry

        lax.fori_loop(0, pieces - 1, drain_relay, 0)


def run(rows, cols, features, first, second, scales):
    chans, height, width = features.shape
    count = height // STEP
    depth = count * chans
    ratio = rows // cols
    slots = (cols - 1) * ratio
    pieces = (chans // PART) * STEP
    full = depth + 2 * chans
    x = jnp.transpose(features.reshape(chans, count, STEP, width), (2, 1, 0, 3))
    x = x.reshape(STEP, depth, width)
    scales = [v.reshape(1, chans) for v in scales]
    vmem = pl.BlockSpec(memory_space=pltpu.VMEM)
    dma = pltpu.SemaphoreType.DMA
    return pl.pallas_call(
        functools.partial(kernel, rows, cols),
        out_shape=jax.ShapeDtypeStruct(features.shape, BF16),
        in_specs=[vmem] * 7,
        out_specs=vmem,
        scratch_shapes=[
            pltpu.VMEM((STEP, full, width), BF16),
            pltpu.VMEM((STEP, full, width), BF16),
            pltpu.VMEM((width // LANES, STEP * depth, LANES), F32),
            pltpu.VMEM((2 * STEP, 2 * LANES, LANES), BF16),
            pltpu.VMEM((2, depth, LANES), F32),
            pltpu.VMEM((2, 3, GROUP * chans, (GROUP + 2) * chans), BF16),
            pltpu.VMEM((2, 2, depth // 2, LANES), BF16),
            pltpu.VMEM((2, 2, depth // 2 + 2 * chans, LANES), BF16),
            pltpu.VMEM((2 * cols, 8, LANES), F32),
            pltpu.VMEM((2 * rows, 8, LANES), F32),
            pltpu.VMEM((STEP, count, chans, width), BF16),
            pltpu.VMEM((STEP, ratio * count, chans, height), BF16),
            pltpu.VMEM((STEP * ratio * depth, height), F32),
            pltpu.VMEM((slots, STEP, count, chans, height), BF16),
            dma((16,)),
            dma((16,)),
            dma((2 * cols,)),
            dma((2 * cols,)),
            dma((2 * rows,)),
            dma((2 * rows,)),
            dma((ratio * pieces,)),
            dma((ratio * pieces,)),
            dma((slots * pieces,)),
            dma((slots * pieces,)),
        ],
        compiler_params=pltpu.CompilerParams(
            collective_id=0, has_side_effects=True, vmem_limit_bytes=44 * 1024 * 1024
        ),
    )(x, first, second, *scales)


def solution(mesh):
    rows, cols = mesh.shape["row"], mesh.shape["col"]

    def per_device(features, first, second, gain_one, shift_one, gain_two, shift_two):
        scales = (gain_one, shift_one, gain_two, shift_two)
        return run(rows, cols, features, first, second, scales)

    placed = (P(None, "row", "col"), P(), P(), P(), P(), P(), P())
    return jax.shard_map(
        per_device, mesh=mesh, in_specs=placed, out_specs=P(None, "row", "col"), check_vma=False
    )
```

```python
import functools

import jax
import jax.numpy as jnp
from jax import lax
from jax.experimental import pallas as pl
from jax.experimental.pallas import tpu as pltpu
from jax.sharding import PartitionSpec as P

STEP = 8
GROUP = 4
EPSILON = 1e-05
LANES = 128
PART = 16
MESH = pl.DeviceIdType.MESH
BF16 = jnp.bfloat16
F32 = jnp.float32

DIRECT = ((0, 1), (0, 2), (1, 3), (2, 0), (3, 1), (3, 2))

WAYS = ((-1, -1), (-1, 0), (-1, 1), (0, -1), (0, 1), (1, -1), (1, 0), (1, 1))


def iota(shape, dim):
    return lax.broadcasted_iota(jnp.int32, shape, dim)


def one_hot(mask):
    return jnp.where(mask, 1.0, 0.0).astype(BF16)


def dot(a, b):
    return jnp.dot(a, b, preferred_element_type=F32)


def remote(src, dst, send, recv, device):
    return pltpu.make_async_remote_copy(
        src_ref=src,
        dst_ref=dst,
        send_sem=send,
        recv_sem=recv,
        device_id=device,
        device_id_type=MESH,
    )


def kernel(
    rows,
    cols,
    x_ref,
    first_ref,
    second_ref,
    gain_one,
    shift_one,
    gain_two,
    shift_two,
    out_ref,
    pad_one,
    pad_two,
    hidden,
    pack_sel,
    edges,
    weights,
    packed,
    strips,
    col_stats,
    row_stats,
    summed,
    got,
    wide,
    relay,
    halo_send,
    halo_recv,
    cs_send,
    cs_recv,
    rs_send,
    rs_recv,
    send,
    recv,
    relay_send,
    relay_recv,
):
    row = lax.axis_index("row")
    col = lax.axis_index("col")
    phases, depth, width = x_ref.shape
    chans, height, _ = out_ref.shape
    count = depth // chans
    full = depth + 2 * chans
    fold_rows = depth // 2
    half_lanes = LANES // 2
    cells = float(phases * count * width)
    ratio = rows // cols
    block = lax.div(row, ratio)
    part = lax.rem(row, ratio)
    relays = block == col
    parts = chans // PART
    pieces = parts * phases

    for pad in (pad_one, pad_two):
        for at, size in ((0, chans), (depth + chans, chans)):
            pad[:, pl.ds(at, size), :] = jnp.zeros((phases, size, width), BF16)
    strips[...] = jnp.zeros_like(strips)

    barrier = pltpu.get_barrier_semaphore()

    def greet(device):
        pl.semaphore_signal(barrier, inc=1, device_id=device, device_id_type=MESH)

    def neighbour(k):
        dr, dc = WAYS[k]
        there = jnp.bool_(True)
        if dr:
            there = there & ((row > 0) if dr < 0 else (row < rows - 1))
        if dc:
            there = there & ((col > 0) if dc < 0 else (col < cols - 1))
        device = (jnp.clip(row + dr, 0, rows - 1), jnp.clip(col + dc, 0, cols - 1))
        return there, device

    expected = jnp.int32(rows + cols - 2)
    for d in range(1, cols):
        greet((row, lax.rem(col + d, cols)))
    for d in range(1, rows):
        greet((lax.rem(row + d, rows), col))
    for k in (0, 2, 5, 7):
        there, device = neighbour(k)
        pl.when(there)(functools.partial(greet, device))
        expected = expected + jnp.where(there, 1, 0)
    for h in range(ratio):
        pl.when(jnp.logical_not(relays))(functools.partial(greet, (ratio * col + h, block)))
    expected = expected + jnp.where(relays, 0, ratio)

    pad_one[:, pl.ds(chans, depth), :] = x_ref[...]

    i, j = iota((2 * LANES, LANES), 0), iota((2 * LANES, LANES), 1)
    edge = LANES - STEP
    lane = i % LANES
    goal = (i // LANES) * half_lanes + lane - j
    head = jnp.where(lane < STEP, goal, -LANES)
    tail = jnp.where(lane >= edge, goal - edge, -LANES)
    for phase in range(phases):
        pack_sel[phase] = one_hot(head == -phase * STEP)
        pack_sel[phases + phase] = one_hot(tail == -phase * STEP)

    def band(n, kernel_ref):
        span = (GROUP + 2) * chans
        c, k = iota((chans, span), 0), iota((chans, span), 1)
        for q in range(GROUP):
            for b in range(3):
                total = jnp.zeros((chans, span), F32)
                for a in range(3):
                    total += dot(kernel_ref[a, b], one_hot(k == c + (q + a) * chans))
                weights[n, b, pl.ds(q * chans, chans), :] = total.astype(BF16)

    pl.semaphore_wait(barrier, expected)

    def halo_copy(pad, n, k):
        dr, dc = WAYS[k]
        there, device = neighbour(k)
        if dc == 0:
            source = chans if dr < 0 else depth
            target = depth + chans if dr < 0 else 0
            src = pad.at[:, pl.ds(source, chans)]
            dst = pad.at[:, pl.ds(target, chans)]
        else:
            mine, theirs = (0, 1) if dc < 0 else (1, 0)
            if dr == 0:
                src = packed.at[n, mine]
                dst = strips.at[n, theirs, pl.ds(0, fold_rows)]
            elif dr < 0:
                src = packed.at[n, mine, pl.ds(0, chans)]
                dst = strips.at[n, theirs, pl.ds(fold_rows + chans, chans)]
            else:
                src = packed.at[n, mine, pl.ds(fold_rows - chans, chans)]
                dst = strips.at[n, theirs, pl.ds(fold_rows, chans)]
        slot = n * 8 + k
        return there, remote(src, dst, halo_send.at[slot], halo_recv.at[slot], device)

    def halo_start(pad, n):
        for k in (1, 6):
            there, copy = halo_copy(pad, n, k)
            pl.when(there)(copy.start)
        for side, lane in ((0, 0), (1, width - LANES)):
            total = jnp.zeros((fold_rows, LANES), F32)
            for phase in range(phases):
                low = pad[phase, pl.ds(chans, fold_rows), pl.ds(lane, LANES)]
                high = pad[phase, pl.ds(chans + fold_rows, fold_rows), pl.ds(lane, LANES)]
                total += dot(
                    jnp.concatenate([low, high], axis=1), pack_sel[side * phases + phase]
                )
            packed[n, side] = total.astype(BF16)
            for k in (3, 0, 5) if side == 0 else (4, 2, 7):
                there, copy = halo_copy(pad, n, k)
                pl.when(there)(copy.start)

    def halo_finish(pad, n):
        for k in range(8):
            there, copy = halo_copy(pad, n, k)
            _, back = halo_copy(pad, n, 7 - k)

            @pl.when(there)
            def _(copy=copy, back=back):
                back.wait_recv()
                copy.wait_send()

    tiles = width // LANES

    def held(at):
        return jnp.concatenate([hidden[k, at, :] for k in range(tiles)], axis=1)

    def keep(at, values):
        for k in range(tiles):
            hidden[k, at, :] = values[:, k * LANES : (k + 1) * LANES]

    def fold(values):
        total = jnp.sum(values.reshape(-1, chans, width), axis=0)
        return sum(total[:, k : k + LANES] for k in range(0, width, LANES))

    def taps(pad, n, groups, acc):
        def body(phase, acc):
            for first, last in groups:
                low = first * GROUP * chans
                rows_in = ((last - first) * GROUP + 2) * chans
                middle = pad[phase, pl.ds(low, rows_in), :]
                blank = jnp.zeros((rows_in, STEP), BF16)
                shifted = (
                    jnp.concatenate([blank, middle[:, : width - STEP]], axis=1),
                    middle,
                    jnp.concatenate([middle[:, STEP:], blank], axis=1),
                )
                for g in range(last - first):
                    at = g * GROUP * chans
                    result = sum(
                        dot(weights[n, b], shifted[b][at : at + (GROUP + 2) * chans])
                        for b in range(3)
                    )
                    keep(pl.ds(phase * depth + low + at, GROUP * chans), result)
                    acc = acc + fold(result)
            return acc

        return lax.fori_loop(0, phases, body, acc, unroll=True)

    lanes = iota((GROUP * chans, LANES), 1)

    def strip_taps(n, side, acc):
        swap = lambda v: jnp.concatenate([v[:, half_lanes:], v[:, :half_lanes]], axis=1)
        whole = strips[n, side, pl.ds(0, fold_rows), :]
        up = strips[n, side, pl.ds(fold_rows, chans), :]
        down = strips[n, side, pl.ds(fold_rows + chans, chans), :]
        column = jnp.concatenate([swap(up), whole, swap(whole), down], axis=0)
        for g in range(count // GROUP):
            low = g * GROUP * chans
            added = dot(weights[n, 2 * side], column[low : low + (GROUP + 2) * chans])
            added = jnp.where(lanes < half_lanes, added, 0.0)
            edges[side, pl.ds(low, GROUP * chans), :] = added
            acc = acc + jnp.sum(added.reshape(GROUP, chans, LANES), axis=0)
        return acc

    def conv(pad, n):
        last = count // GROUP
        acc = taps(pad, n, ((1, last - 1),), jnp.zeros((chans, LANES), F32))
        halo_finish(pad, n)
        acc = taps(pad, n, ((0, 1), (last - 1, last)), acc)
        for side in range(2):
            acc = strip_taps(n, side, acc)
        return acc

    square = (chans, LANES)
    diagonal = iota(square, 0) == iota(square, 1)

    def to_lanes(values):
        return jnp.sum(jnp.where(diagonal, values, 0.0), axis=0, keepdims=True)

    def to_rows(values):
        spread = jnp.where(diagonal, jnp.broadcast_to(values, square), 0.0)
        return jnp.broadcast_to(jnp.sum(spread, axis=1, keepdims=True), square)

    def merge(own, other, size, stats, sends, recvs, n, axis_size, along_row):
        base = n * axis_size
        stats[base, pl.ds(0, 1), :] = own
        stats[base, pl.ds(1, 1), :] = other
        copies = []
        for d in range(1, axis_size):
            device = (
                (lax.rem(row + d, axis_size), col)
                if along_row
                else (row, lax.rem(col + d, axis_size))
            )
            copy = remote(
                stats.at[base],
                stats.at[base + d],
                sends.at[base + d],
                recvs.at[base + d],
                device,
            )
            copy.start()
            copies.append(copy)
        for copy in copies:
            copy.wait()
        means = [stats[base + d, pl.ds(0, 1), :] for d in range(axis_size)]
        mean = sum(means) / axis_size
        squares = sum(stats[base + d, pl.ds(1, 1), :] for d in range(axis_size))
        spread = sum((m - mean) * (m - mean) for m in means)
        return mean, squares + size * spread

    def norm(acc, n, gain, shift):
        own = jnp.broadcast_to(jnp.sum(acc, axis=1, keepdims=True) / cells, square)
        across = jnp.concatenate([own] * GROUP, axis=0)
        squares = jnp.zeros(square, F32)
        for phase in range(phases):
            for g in range(count // GROUP):
                low = g * GROUP * chans
                at = pl.ds(phase * depth + low, GROUP * chans)
                for k in range(tiles):
                    cell = hidden[k, at, :]
                    for side, tile, start in ((0, 0, 0), (1, tiles - 1, edge)):
                        if k == tile:
                            moved = pltpu.roll(
                                edges[side, pl.ds(low, GROUP * chans), :],
                                (start - phase * STEP) % LANES,
                                1,
                            )
                            wanted = lanes >= edge if side else lanes < STEP
                            cell = cell + jnp.where(wanted, moved, 0.0)
                            hidden[k, at, :] = cell
                    diff = cell - across
                    diff = (diff * diff).reshape(GROUP, chans, LANES)
                    squares = squares + jnp.sum(diff, axis=0)
        squares = jnp.broadcast_to(jnp.sum(squares, axis=1, keepdims=True), square)
        mean, squares = merge(
            to_lanes(own), to_lanes(squares), cells, col_stats, cs_send, cs_recv, n, cols, False
        )
        mean, squares = merge(
            mean, squares, cells * cols, row_stats, rs_send, rs_recv, n, rows, True
        )
        blank = jnp.zeros((1, LANES - chans), F32)
        gains = jnp.concatenate([gain[...], blank], axis=1)
        shifts = jnp.concatenate([shift[...], blank], axis=1)
        factor = gains * lax.rsqrt(squares / (cells * (rows * cols)) + EPSILON)
        repeat = lambda v: jnp.concatenate([to_rows(v)] * (width // LANES), axis=1)
        return repeat(mean), repeat(factor), repeat(shifts)

    halo_start(pad_one, 0)
    band(0, first_ref)
    band(1, second_ref)
    mean, factor, shift = norm(conv(pad_one, 0), 0, gain_one, shift_one)

    def activate(phase, carry):
        for q in range(count):
            cell = held(pl.ds(phase * depth + q * chans, chans))
            cell = jnp.maximum((cell - mean) * factor + shift, 0.0)
            pad_two[phase, pl.ds((q + 1) * chans, chans), :] = cell.astype(BF16)
        return carry

    lax.fori_loop(0, phases, activate, 0)
    halo_start(pad_two, 1)
    mean, factor, shift = norm(conv(pad_two, 1), 1, gain_two, shift_two)

    def direct(source_col, source_block):
        z, p = lax.rem(source_col, 4), lax.rem(source_block, 4)
        chosen = (z == p) & (lax.rem(source_col + source_block, 8) < 4)
        for a, b in DIRECT:
            chosen = chosen | ((z == a) & (p == b))
        return chosen

    mine = direct(col, block)

    def crosses(target):
        return (2 * col < cols) != (2 * target < cols)

    def passes(d, k):
        target = lax.rem(col + d, cols)
        straight_on = (k == pieces - 1) & crosses(target)
        return jnp.logical_not(direct(col, target) | straight_on)

    def band_of(k):
        return pl.ds(pl.multiple_of((k // phases) * PART, PART), PART)

    def source(h, k):
        return summed.at[k % phases, :, band_of(k), pl.ds(h * height, height)]

    def landing(e, k):
        return got.at[k % phases, pl.ds(e * count, count), band_of(k), :]

    def waypoint(slot, k):
        return relay.at[slot, k % phases, :, band_of(k), :]

    def straight(h, k):
        return remote(
            source(h, k),
            landing(part, k),
            send.at[h * pieces + k],
            recv.at[part * pieces + k],
            (ratio * col + h, block),
        )

    def arrive(e, k):
        return remote(
            landing(e, k),
            landing(e, k),
            send.at[e * pieces + k],
            recv.at[e * pieces + k],
            (row, col),
        )

    def first_leg(h, k):
        slot = (lax.rem(block - col + cols, cols) - 1) * ratio + part
        return remote(
            source(h, k),
            waypoint(slot, k),
            send.at[h * pieces + k],
            relay_recv.at[slot * pieces + k],
            (ratio * col + h, col),
        )

    def second_leg(d, e, k):
        slot = (d - 1) * ratio + e
        return remote(
            waypoint(slot, k),
            landing(e, k),
            relay_send.at[slot * pieces + k],
            recv.at[e * pieces + k],
            (row, lax.rem(col + d, cols)),
        )

    def issue(k):
        goes = relays | mine | ((k == pieces - 1) & crosses(block))
        for h in range(ratio):
            here = relays & (part == h)

            @pl.when(goes & jnp.logical_not(here))
            def _(h=h):
                straight(h, k).start()

            @pl.when(jnp.logical_not(goes))
            def _(h=h):
                first_leg(h, k).start()

    def finish(phase, carry):
        for q in range(count):
            at = pl.ds(phase * depth + q * chans, chans)
            cell = (held(at) - mean) * factor + shift
            cell = (x_ref[phase, pl.ds(q * chans, chans), :].astype(F32) + cell).astype(BF16)
            summed[phase, q] = cell
            keep(at, cell.astype(F32))
        issue(phase)
        return carry

    lax.fori_loop(0, phases, finish, 0)

    def issue_rest(k, carry):
        issue(k)
        return carry

    lax.fori_loop(phases, pieces, issue_rest, 0)

    @pl.when(relays)
    def _():
        for h in range(ratio):

            @pl.when(part == h)
            def _(h=h):
                got[:, pl.ds(h * count, count), :, :] = summed[
                    :, :, :, pl.ds(h * height, height)
                ]

    def forward(k, carry):
        for d in range(1, cols):

            @pl.when(passes(d, k))
            def _(d=d):
                for e in range(ratio):
                    slot = (d - 1) * ratio + e
                    remote(
                        waypoint(slot, k),
                        waypoint(slot, k),
                        relay_send.at[slot * pieces + k],
                        relay_recv.at[slot * pieces + k],
                        (row, col),
                    ).wait_recv()
                    second_leg(d, e, k).start()

        return carry

    span = ratio * depth
    unit = one_hot(iota((height, height), 0) == iota((height, height), 1))
    for p in range(parts):

        @pl.when(relays)
        def _(p=p):
            lax.fori_loop(p * phases, (p + 1) * phases, forward, 0)

        def collect(phase, carry, p=p):
            k = p * phases + phase
            for e in range(ratio):

                @pl.when(jnp.logical_not(relays & (part == e)))
                def _(e=e):
                    arrive(e, k).wait_recv()

            for q in range(ratio * count):
                wide[pl.ds(phase * span + q * chans + p * PART, PART), :] = got[
                    phase, q, pl.ds(p * PART, PART), :
                ].astype(F32)
            return carry

        lax.fori_loop(0, phases, collect, 0)

        def turn(c, carry):
            own = jnp.concatenate(
                [
                    held(pl.ds(q * chans + c, phases, stride=depth))
                    for q in range(count)
                ],
                axis=0,
            )
            other = jnp.concatenate(
                [
                    wide[pl.ds(q * chans + c, phases, stride=span), :]
                    for q in range(ratio * count)
                ],
                axis=0,
            )
            total = own + lax.dot_general(
                unit, other.astype(BF16), (((1,), (1,)), ((), ())), preferred_element_type=F32
            )
            out_ref[c] = (total * 0.5).astype(BF16)
            return carry

        lax.fori_loop(p * PART, (p + 1) * PART, turn, 0, unroll=4)

    def drain(k, carry):
        for h in range(ratio):

            @pl.when(jnp.logical_not(relays & (part == h)))
            def _(h=h):
                straight(h, k).wait_send()

        return carry

    lax.fori_loop(0, pieces, drain, 0)

    @pl.when(relays)
    def _():
        def drain_relay(k, carry):
            for d in range(1, cols):

                @pl.when(passes(d, k))
                def _(d=d):
                    for e in range(ratio):
                        second_leg(d, e, k).wait_send()

            return carry

        lax.fori_loop(0, pieces, drain_relay, 0)


def run(rows, cols, features, first, second, scales):
    chans, height, width = features.shape
    count = height // STEP
    depth = count * chans
    ratio = rows // cols
    slots = (cols - 1) * ratio
    pieces = (chans // PART) * STEP
    full = depth + 2 * chans
    x = jnp.transpose(features.reshape(chans, count, STEP, width), (2, 1, 0, 3))
    x = x.reshape(STEP, depth, width)
    scales = [v.reshape(1, chans) for v in scales]
    vmem = pl.BlockSpec(memory_space=pltpu.VMEM)
    dma = pltpu.SemaphoreType.DMA
    return pl.pallas_call(
        functools.partial(kernel, rows, cols),
        out_shape=jax.ShapeDtypeStruct(features.shape, BF16),
        in_specs=[vmem] * 7,
        out_specs=vmem,
        scratch_shapes=[
            pltpu.VMEM((STEP, full, width), BF16),
            pltpu.VMEM((STEP, full, width), BF16),
            pltpu.VMEM((width // LANES, STEP * depth, LANES), F32),
            pltpu.VMEM((2 * STEP, 2 * LANES, LANES), BF16),
            pltpu.VMEM((2, depth, LANES), F32),
            pltpu.VMEM((2, 3, GROUP * chans, (GROUP + 2) * chans), BF16),
            pltpu.VMEM((2, 2, depth // 2, LANES), BF16),
            pltpu.VMEM((2, 2, depth // 2 + 2 * chans, LANES), BF16),
            pltpu.VMEM((2 * cols, 8, LANES), F32),
            pltpu.VMEM((2 * rows, 8, LANES), F32),
            pltpu.VMEM((STEP, count, chans, width), BF16),
            pltpu.VMEM((STEP, ratio * count, chans, height), BF16),
            pltpu.VMEM((STEP * ratio * depth, height), F32),
            pltpu.VMEM((slots, STEP, count, chans, height), BF16),
            dma((16,)),
            dma((16,)),
            dma((2 * cols,)),
            dma((2 * cols,)),
            dma((2 * rows,)),
            dma((2 * rows,)),
            dma((ratio * pieces,)),
            dma((ratio * pieces,)),
            dma((slots * pieces,)),
            dma((slots * pieces,)),
        ],
        compiler_params=pltpu.CompilerParams(
            collective_id=0, has_side_effects=True, vmem_limit_bytes=44 * 1024 * 1024
        ),
    )(x, first, second, *scales)


def solution(mesh):
    rows, cols = mesh.shape["row"], mesh.shape["col"]

    def per_device(features, first, second, gain_one, shift_one, gain_two, shift_two):
        scales = (gain_one, shift_one, gain_two, shift_two)
        return run(rows, cols, features, first, second, scales)

    placed = (P(None, "row", "col"), P(), P(), P(), P(), P(), P())
    return jax.shard_map(
        per_device, mesh=mesh, in_specs=placed, out_specs=P(None, "row", "col"), check_vma=False
    )
```

```python
import functools

import jax
import jax.numpy as jnp
from jax import lax
from jax.experimental import pallas as pl
from jax.experimental.pallas import tpu as pltpu
from jax.sharding import PartitionSpec as P

STEP = 8
GROUP = 4
EPSILON = 1e-05
LANES = 128
PART = 16
MESH = pl.DeviceIdType.MESH
BF16 = jnp.bfloat16
F32 = jnp.float32

DIRECT = ((0, 1), (0, 2), (1, 3), (2, 0), (3, 1), (3, 2))

WAYS = ((-1, -1), (-1, 0), (-1, 1), (0, -1), (0, 1), (1, -1), (1, 0), (1, 1))


def iota(shape, dim):
    return lax.broadcasted_iota(jnp.int32, shape, dim)


def one_hot(mask):
    return jnp.where(mask, 1.0, 0.0).astype(BF16)


def dot(a, b):
    return jnp.dot(a, b, preferred_element_type=F32)


def piece_table(parts):
    table = []
    for p in range(parts):
        sizes = (1, 1, 2, 2, 2) if p < parts - 1 else (2, 2, 2, 1, 1)
        at = 0
        for size in sizes:
            table.append((p, at, size))
            at += size
    return table


def remote(src, dst, send, recv, device):
    return pltpu.make_async_remote_copy(
        src_ref=src,
        dst_ref=dst,
        send_sem=send,
        recv_sem=recv,
        device_id=device,
        device_id_type=MESH,
    )


def kernel(
    rows,
    cols,
    x_ref,
    first_ref,
    second_ref,
    gain_one,
    shift_one,
    gain_two,
    shift_two,
    out_ref,
    pad_one,
    pad_two,
    hidden,
    pack_sel,
    edges,
    weights,
    packed,
    strips,
    col_stats,
    row_stats,
    summed,
    got,
    wide,
    relay,
    halo_send,
    halo_recv,
    cs_send,
    cs_recv,
    rs_send,
    rs_recv,
    send,
    recv,
    relay_send,
    relay_recv,
):
    row = lax.axis_index("row")
    col = lax.axis_index("col")
    phases, depth, width = x_ref.shape
    chans, height, _ = out_ref.shape
    count = depth // chans
    full = depth + 2 * chans
    fold_rows = depth // 2
    half_lanes = LANES // 2
    cells = float(phases * count * width)
    ratio = rows // cols
    block = lax.div(row, ratio)
    part = lax.rem(row, ratio)
    relays = block == col
    parts = chans // PART
    table = piece_table(parts)
    pieces = len(table)
    of_part = lambda p: [k for k in range(pieces) if table[k][0] == p]

    for pad in (pad_one, pad_two):
        for at, size in ((0, chans), (depth + chans, chans)):
            pad[:, pl.ds(at, size), :] = jnp.zeros((phases, size, width), BF16)
    strips[...] = jnp.zeros_like(strips)

    barrier = pltpu.get_barrier_semaphore()

    def greet(device):
        pl.semaphore_signal(barrier, inc=1, device_id=device, device_id_type=MESH)

    def neighbour(k):
        dr, dc = WAYS[k]
        there = jnp.bool_(True)
        if dr:
            there = there & ((row > 0) if dr < 0 else (row < rows - 1))
        if dc:
            there = there & ((col > 0) if dc < 0 else (col < cols - 1))
        device = (jnp.clip(row + dr, 0, rows - 1), jnp.clip(col + dc, 0, cols - 1))
        return there, device

    expected = jnp.int32(rows + cols - 2)
    for d in range(1, cols):
        greet((row, lax.rem(col + d, cols)))
    for d in range(1, rows):
        greet((lax.rem(row + d, rows), col))
    for k in (0, 2, 5, 7):
        there, device = neighbour(k)
        pl.when(there)(functools.partial(greet, device))
        expected = expected + jnp.where(there, 1, 0)
    for h in range(ratio):
        pl.when(jnp.logical_not(relays))(functools.partial(greet, (ratio * col + h, block)))
    expected = expected + jnp.where(relays, 0, ratio)

    pad_one[:, pl.ds(chans, depth), :] = x_ref[...]

    i, j = iota((2 * LANES, LANES), 0), iota((2 * LANES, LANES), 1)
    edge = LANES - STEP
    lane = i % LANES
    goal = (i // LANES) * half_lanes + lane - j
    head = jnp.where(lane < STEP, goal, -LANES)
    tail = jnp.where(lane >= edge, goal - edge, -LANES)
    for phase in range(phases):
        pack_sel[phase] = one_hot(head == -phase * STEP)
        pack_sel[phases + phase] = one_hot(tail == -phase * STEP)

    def band(n, kernel_ref):
        span = (GROUP + 2) * chans
        c, k = iota((chans, span), 0), iota((chans, span), 1)
        for q in range(GROUP):
            for b in range(3):
                total = jnp.zeros((chans, span), F32)
                for a in range(3):
                    total += dot(kernel_ref[a, b], one_hot(k == c + (q + a) * chans))
                weights[n, b, pl.ds(q * chans, chans), :] = total.astype(BF16)

    pl.semaphore_wait(barrier, expected)

    def halo_copy(pad, n, k):
        dr, dc = WAYS[k]
        there, device = neighbour(k)
        if dc == 0:
            source = chans if dr < 0 else depth
            target = depth + chans if dr < 0 else 0
            src = pad.at[:, pl.ds(source, chans)]
            dst = pad.at[:, pl.ds(target, chans)]
        else:
            mine, theirs = (0, 1) if dc < 0 else (1, 0)
            if dr == 0:
                src = packed.at[n, mine]
                dst = strips.at[n, theirs, pl.ds(0, fold_rows)]
            elif dr < 0:
                src = packed.at[n, mine, pl.ds(0, chans)]
                dst = strips.at[n, theirs, pl.ds(fold_rows + chans, chans)]
            else:
                src = packed.at[n, mine, pl.ds(fold_rows - chans, chans)]
                dst = strips.at[n, theirs, pl.ds(fold_rows, chans)]
        slot = n * 8 + k
        return there, remote(src, dst, halo_send.at[slot], halo_recv.at[slot], device)

    def halo_start(pad, n):
        for k in (1, 6):
            there, copy = halo_copy(pad, n, k)
            pl.when(there)(copy.start)
        for side, lane in ((0, 0), (1, width - LANES)):
            total = jnp.zeros((fold_rows, LANES), F32)
            for phase in range(phases):
                low = pad[phase, pl.ds(chans, fold_rows), pl.ds(lane, LANES)]
                high = pad[phase, pl.ds(chans + fold_rows, fold_rows), pl.ds(lane, LANES)]
                total += dot(
                    jnp.concatenate([low, high], axis=1), pack_sel[side * phases + phase]
                )
            packed[n, side] = total.astype(BF16)
            for k in (3, 0, 5) if side == 0 else (4, 2, 7):
                there, copy = halo_copy(pad, n, k)
                pl.when(there)(copy.start)

    def halo_finish(pad, n):
        for k in range(8):
            there, copy = halo_copy(pad, n, k)
            _, back = halo_copy(pad, n, 7 - k)

            @pl.when(there)
            def _(copy=copy, back=back):
                back.wait_recv()
                copy.wait_send()

    tiles = width // LANES

    def held(at):
        return jnp.concatenate([hidden[k, at, :] for k in range(tiles)], axis=1)

    def keep(at, values):
        for k in range(tiles):
            hidden[k, at, :] = values[:, k * LANES : (k + 1) * LANES]

    def fold(values):
        total = jnp.sum(values.reshape(-1, chans, width), axis=0)
        return sum(total[:, k : k + LANES] for k in range(0, width, LANES))

    def taps(pad, n, groups, acc):
        def body(phase, acc):
            for first, last in groups:
                low = first * GROUP * chans
                rows_in = ((last - first) * GROUP + 2) * chans
                middle = pad[phase, pl.ds(low, rows_in), :]
                blank = jnp.zeros((rows_in, STEP), BF16)
                shifted = (
                    jnp.concatenate([blank, middle[:, : width - STEP]], axis=1),
                    middle,
                    jnp.concatenate([middle[:, STEP:], blank], axis=1),
                )
                for g in range(last - first):
                    at = g * GROUP * chans
                    result = sum(
                        dot(weights[n, b], shifted[b][at : at + (GROUP + 2) * chans])
                        for b in range(3)
                    )
                    keep(pl.ds(phase * depth + low + at, GROUP * chans), result)
                    acc = acc + fold(result)
            return acc

        return lax.fori_loop(0, phases, body, acc, unroll=True)

    lanes = iota((GROUP * chans, LANES), 1)

    def strip_taps(n, side, acc):
        swap = lambda v: jnp.concatenate([v[:, half_lanes:], v[:, :half_lanes]], axis=1)
        whole = strips[n, side, pl.ds(0, fold_rows), :]
        up = strips[n, side, pl.ds(fold_rows, chans), :]
        down = strips[n, side, pl.ds(fold_rows + chans, chans), :]
        column = jnp.concatenate([swap(up), whole, swap(whole), down], axis=0)
        for g in range(count // GROUP):
            low = g * GROUP * chans
            added = dot(weights[n, 2 * side], column[low : low + (GROUP + 2) * chans])
            added = jnp.where(lanes < half_lanes, added, 0.0)
            edges[side, pl.ds(low, GROUP * chans), :] = added
            acc = acc + jnp.sum(added.reshape(GROUP, chans, LANES), axis=0)
        return acc

    def conv(pad, n):
        last = count // GROUP
        acc = taps(pad, n, ((1, last - 1),), jnp.zeros((chans, LANES), F32))
        halo_finish(pad, n)
        acc = taps(pad, n, ((0, 1), (last - 1, last)), acc)
        for side in range(2):
            acc = strip_taps(n, side, acc)
        return acc

    square = (chans, LANES)
    diagonal = iota(square, 0) == iota(square, 1)

    def to_lanes(values):
        return jnp.sum(jnp.where(diagonal, values, 0.0), axis=0, keepdims=True)

    def to_rows(values):
        spread = jnp.where(diagonal, jnp.broadcast_to(values, square), 0.0)
        return jnp.broadcast_to(jnp.sum(spread, axis=1, keepdims=True), square)

    def merge(own, other, size, stats, sends, recvs, n, axis_size, along_row):
        base = n * axis_size
        stats[base, pl.ds(0, 1), :] = own
        stats[base, pl.ds(1, 1), :] = other
        copies = []
        for d in range(1, axis_size):
            device = (
                (lax.rem(row + d, axis_size), col)
                if along_row
                else (row, lax.rem(col + d, axis_size))
            )
            copy = remote(
                stats.at[base],
                stats.at[base + d],
                sends.at[base + d],
                recvs.at[base + d],
                device,
            )
            copy.start()
            copies.append(copy)
        for copy in copies:
            copy.wait()
        means = [stats[base + d, pl.ds(0, 1), :] for d in range(axis_size)]
        mean = sum(means) / axis_size
        squares = sum(stats[base + d, pl.ds(1, 1), :] for d in range(axis_size))
        spread = sum((m - mean) * (m - mean) for m in means)
        return mean, squares + size * spread

    def norm(acc, n, gain, shift):
        own = jnp.broadcast_to(jnp.sum(acc, axis=1, keepdims=True) / cells, square)
        across = jnp.concatenate([own] * GROUP, axis=0)
        squares = jnp.zeros(square, F32)
        for phase in range(phases):
            for g in range(count // GROUP):
                low = g * GROUP * chans
                at = pl.ds(phase * depth + low, GROUP * chans)
                for k in range(tiles):
                    cell = hidden[k, at, :]
                    for side, tile, start in ((0, 0, 0), (1, tiles - 1, edge)):
                        if k == tile:
                            moved = pltpu.roll(
                                edges[side, pl.ds(low, GROUP * chans), :],
                                (start - phase * STEP) % LANES,
                                1,
                            )
                            wanted = lanes >= edge if side else lanes < STEP
                            cell = cell + jnp.where(wanted, moved, 0.0)
                            hidden[k, at, :] = cell
                    diff = cell - across
                    diff = (diff * diff).reshape(GROUP, chans, LANES)
                    squares = squares + jnp.sum(diff, axis=0)
        squares = jnp.broadcast_to(jnp.sum(squares, axis=1, keepdims=True), square)
        mean, squares = merge(
            to_lanes(own), to_lanes(squares), cells, col_stats, cs_send, cs_recv, n, cols, False
        )
        mean, squares = merge(
            mean, squares, cells * cols, row_stats, rs_send, rs_recv, n, rows, True
        )
        blank = jnp.zeros((1, LANES - chans), F32)
        gains = jnp.concatenate([gain[...], blank], axis=1)
        shifts = jnp.concatenate([shift[...], blank], axis=1)
        factor = gains * lax.rsqrt(squares / (cells * (rows * cols)) + EPSILON)
        repeat = lambda v: jnp.concatenate([to_rows(v)] * (width // LANES), axis=1)
        return repeat(mean), repeat(factor), repeat(shifts)

    halo_start(pad_one, 0)
    band(0, first_ref)
    band(1, second_ref)
    mean, factor, shift = norm(conv(pad_one, 0), 0, gain_one, shift_one)

    def activate(phase, carry):
        for q in range(count):
            cell = held(pl.ds(phase * depth + q * chans, chans))
            cell = jnp.maximum((cell - mean) * factor + shift, 0.0)
            pad_two[phase, pl.ds((q + 1) * chans, chans), :] = cell.astype(BF16)
        return carry

    lax.fori_loop(0, phases, activate, 0)
    halo_start(pad_two, 1)
    mean, factor, shift = norm(conv(pad_two, 1), 1, gain_two, shift_two)

    def direct(source_col, source_block):
        z, p = lax.rem(source_col, 4), lax.rem(source_block, 4)
        chosen = (z == p) & (lax.rem(source_col + source_block, 8) < 4)
        for a, b in DIRECT:
            chosen = chosen | ((z == a) & (p == b))
        return chosen

    mine = direct(col, block)

    def crosses(target):
        return (2 * col < cols) != (2 * target < cols)

    def passes(d, k):
        target = lax.rem(col + d, cols)
        straight_on = direct(col, target)
        if k == pieces - 1:
            straight_on = straight_on | crosses(target) | (part == ratio - 1)
        return jnp.logical_not(straight_on)

    def span_of(k):
        p, at, size = table[k]
        return p, pl.ds(at, size)

    def source(h, k):
        return summed.at[(h, *span_of(k))]

    def landing(e, k):
        return got.at[(*span_of(k), pl.ds(e * count, count))]

    def waypoint(slot, k):
        return relay.at[(slot, *span_of(k))]

    def straight(h, k):
        return remote(
            source(h, k),
            landing(part, k),
            send.at[h * pieces + k],
            recv.at[part * pieces + k],
            (ratio * col + h, block),
        )

    def arrive(e, k):
        return remote(
            landing(e, k),
            landing(e, k),
            send.at[e * pieces + k],
            recv.at[e * pieces + k],
            (row, col),
        )

    def first_leg(h, k):
        slot = (lax.rem(block - col + cols, cols) - 1) * ratio + part
        return remote(
            source(h, k),
            waypoint(slot, k),
            send.at[h * pieces + k],
            relay_recv.at[slot * pieces + k],
            (ratio * col + h, col),
        )

    def second_leg(d, e, k):
        slot = (d - 1) * ratio + e
        return remote(
            waypoint(slot, k),
            landing(e, k),
            relay_send.at[slot * pieces + k],
            recv.at[e * pieces + k],
            (row, lax.rem(col + d, cols)),
        )

    def issue(k):
        for h in range(ratio):
            goes = relays | mine
            if k == pieces - 1:
                goes = goes | crosses(block) | (h == ratio - 1)
            here = relays & (part == h)

            @pl.when(goes & jnp.logical_not(here))
            def _(h=h):
                straight(h, k).start()

            @pl.when(jnp.logical_not(goes))
            def _(h=h):
                first_leg(h, k).start()

    def finish(phase, carry):
        for q in range(count):
            at = pl.ds(phase * depth + q * chans, chans)
            cell = (held(at) - mean) * factor + shift
            cell = (x_ref[phase, pl.ds(q * chans, chans), :].astype(F32) + cell).astype(BF16)
            for h in range(ratio):
                for p in range(parts):
                    summed[h, p, phase, q] = cell[
                        p * PART : (p + 1) * PART, h * height : (h + 1) * height
                    ]
            keep(at, cell.astype(F32))
        return carry

    for k in of_part(0):
        _, at, size = table[k]
        lax.fori_loop(at, at + size, finish, 0)
        issue(k)
    for k in range(len(of_part(0)), pieces):
        issue(k)

    @pl.when(relays)
    def _():
        for h in range(ratio):

            @pl.when(part == h)
            def _(h=h):
                got[:, :, pl.ds(h * count, count)] = summed[h]

    def forward(k):
        for d in range(1, cols):

            @pl.when(passes(d, k))
            def _(d=d):
                for e in range(ratio):
                    slot = (d - 1) * ratio + e
                    remote(
                        waypoint(slot, k),
                        waypoint(slot, k),
                        relay_send.at[slot * pieces + k],
                        relay_recv.at[slot * pieces + k],
                        (row, col),
                    ).wait_recv()
                    second_leg(d, e, k).start()

    def drain(k):
        for h in range(ratio):

            @pl.when(jnp.logical_not(relays & (part == h)))
            def _(h=h):
                straight(h, k).wait_send()

    span = ratio * depth
    unit = one_hot(iota((height, height), 0) == iota((height, height), 1))
    for p in range(parts):

        @pl.when(relays)
        def _(p=p):
            for k in of_part(p):
                forward(k)

        if p > 0:
            for k in of_part(p - 1):
                drain(k)

        def collect(phase, carry, p=p):
            for q in range(ratio * count):
                wide[pl.ds(phase * span + q * chans + p * PART, PART), :] = got[
                    p, phase, q
                ].astype(F32)
            return carry

        for k in of_part(p):
            for e in range(ratio):

                @pl.when(jnp.logical_not(relays & (part == e)))
                def _(e=e, k=k):
                    arrive(e, k).wait_recv()

            _, at, size = table[k]
            lax.fori_loop(at, at + size, collect, 0)

        def turn(c, carry):
            own = jnp.concatenate(
                [
                    held(pl.ds(q * chans + c, phases, stride=depth))
                    for q in range(count)
                ],
                axis=0,
            )
            other = jnp.concatenate(
                [
                    wide[pl.ds(q * chans + c, phases, stride=span), :]
                    for q in range(ratio * count)
                ],
                axis=0,
            )
            total = own + lax.dot_general(
                unit, other.astype(BF16), (((1,), (1,)), ((), ())), preferred_element_type=F32
            )
            out_ref[c] = (total * 0.5).astype(BF16)
            return carry

        lax.fori_loop(p * PART, (p + 1) * PART, turn, 0, unroll=4)

    for k in of_part(parts - 1):
        drain(k)

    @pl.when(relays)
    def _():
        for k in range(pieces):
            for d in range(1, cols):

                @pl.when(passes(d, k))
                def _(d=d, k=k):
                    for e in range(ratio):
                        second_leg(d, e, k).wait_send()


def run(rows, cols, features, first, second, scales):
    chans, height, width = features.shape
    count = height // STEP
    depth = count * chans
    ratio = rows // cols
    slots = (cols - 1) * ratio
    parts = chans // PART
    pieces = len(piece_table(parts))
    full = depth + 2 * chans
    x = jnp.transpose(features.reshape(chans, count, STEP, width), (2, 1, 0, 3))
    x = x.reshape(STEP, depth, width)
    scales = [v.reshape(1, chans) for v in scales]
    vmem = pl.BlockSpec(memory_space=pltpu.VMEM)
    dma = pltpu.SemaphoreType.DMA
    return pl.pallas_call(
        functools.partial(kernel, rows, cols),
        out_shape=jax.ShapeDtypeStruct(features.shape, BF16),
        in_specs=[vmem] * 7,
        out_specs=vmem,
        scratch_shapes=[
            pltpu.VMEM((STEP, full, width), BF16),
            pltpu.VMEM((STEP, full, width), BF16),
            pltpu.VMEM((width // LANES, STEP * depth, LANES), F32),
            pltpu.VMEM((2 * STEP, 2 * LANES, LANES), BF16),
            pltpu.VMEM((2, depth, LANES), F32),
            pltpu.VMEM((2, 3, GROUP * chans, (GROUP + 2) * chans), BF16),
            pltpu.VMEM((2, 2, depth // 2, LANES), BF16),
            pltpu.VMEM((2, 2, depth // 2 + 2 * chans, LANES), BF16),
            pltpu.VMEM((2 * cols, 8, LANES), F32),
            pltpu.VMEM((2 * rows, 8, LANES), F32),
            pltpu.VMEM((ratio, parts, STEP, count, PART, height), BF16),
            pltpu.VMEM((parts, STEP, ratio * count, PART, height), BF16),
            pltpu.VMEM((STEP * ratio * depth, height), F32),
            pltpu.VMEM((slots, parts, STEP, count, PART, height), BF16),
            dma((16,)),
            dma((16,)),
            dma((2 * cols,)),
            dma((2 * cols,)),
            dma((2 * rows,)),
            dma((2 * rows,)),
            dma((ratio * pieces,)),
            dma((ratio * pieces,)),
            dma((slots * pieces,)),
            dma((slots * pieces,)),
        ],
        compiler_params=pltpu.CompilerParams(
            collective_id=0, has_side_effects=True, vmem_limit_bytes=44 * 1024 * 1024
        ),
    )(x, first, second, *scales)


def solution(mesh):
    rows, cols = mesh.shape["row"], mesh.shape["col"]

    def per_device(features, first, second, gain_one, shift_one, gain_two, shift_two):
        scales = (gain_one, shift_one, gain_two, shift_two)
        return run(rows, cols, features, first, second, scales)

    placed = (P(None, "row", "col"), P(), P(), P(), P(), P(), P())
    return jax.shard_map(
        per_device, mesh=mesh, in_specs=placed, out_specs=P(None, "row", "col"), check_vma=False
    )
```

```python
import functools

import jax
import jax.numpy as jnp
from jax import lax
from jax.experimental import pallas as pl
from jax.experimental.pallas import tpu as pltpu
from jax.sharding import PartitionSpec as P

STEP = 8
GROUP = 4
EPSILON = 1e-05
LANES = 128
PART = 16
MESH = pl.DeviceIdType.MESH
BF16 = jnp.bfloat16
F32 = jnp.float32

DIRECT = ((0, 1), (0, 2), (1, 3), (2, 0), (3, 1), (3, 2))

WAYS = ((-1, -1), (-1, 0), (-1, 1), (0, -1), (0, 1), (1, -1), (1, 0), (1, 1))


def iota(shape, dim):
    return lax.broadcasted_iota(jnp.int32, shape, dim)


def one_hot(mask):
    return jnp.where(mask, 1.0, 0.0).astype(BF16)


def dot(a, b):
    return jnp.dot(a, b, preferred_element_type=F32)


def piece_table(parts):
    table = []
    for p in range(parts):
        sizes = (1, 1, 2, 2, 2) if p < parts - 1 else (2, 2, 2, 1, 1)
        at = 0
        for size in sizes:
            table.append((p, at, size))
            at += size
    return table


def remote(src, dst, send, recv, device):
    return pltpu.make_async_remote_copy(
        src_ref=src,
        dst_ref=dst,
        send_sem=send,
        recv_sem=recv,
        device_id=device,
        device_id_type=MESH,
    )


def kernel(
    rows,
    cols,
    x_ref,
    first_ref,
    second_ref,
    gain_one,
    shift_one,
    gain_two,
    shift_two,
    out_ref,
    pad_one,
    pad_two,
    hidden,
    pack_sel,
    edges,
    weights,
    packed,
    strips,
    col_stats,
    row_stats,
    summed,
    got,
    wide,
    relay,
    halo_send,
    halo_recv,
    cs_send,
    cs_recv,
    rs_send,
    rs_recv,
    send,
    recv,
    relay_send,
    relay_recv,
):
    row = lax.axis_index("row")
    col = lax.axis_index("col")
    phases, depth, width = x_ref.shape
    chans, height, _ = out_ref.shape
    count = depth // chans
    full = depth + 2 * chans
    fold_rows = depth // 2
    half_lanes = LANES // 2
    cells = float(phases * count * width)
    ratio = rows // cols
    block = lax.div(row, ratio)
    part = lax.rem(row, ratio)
    relays = block == col
    parts = chans // PART
    table = piece_table(parts)
    pieces = len(table)
    of_part = lambda p: [k for k in range(pieces) if table[k][0] == p]

    for pad in (pad_one, pad_two):
        for at, size in ((0, chans), (depth + chans, chans)):
            pad[:, pl.ds(at, size), :] = jnp.zeros((phases, size, width), BF16)
    strips[...] = jnp.zeros_like(strips)

    barrier = pltpu.get_barrier_semaphore()

    def greet(device):
        pl.semaphore_signal(barrier, inc=1, device_id=device, device_id_type=MESH)

    def neighbour(k):
        dr, dc = WAYS[k]
        there = jnp.bool_(True)
        if dr:
            there = there & ((row > 0) if dr < 0 else (row < rows - 1))
        if dc:
            there = there & ((col > 0) if dc < 0 else (col < cols - 1))
        device = (jnp.clip(row + dr, 0, rows - 1), jnp.clip(col + dc, 0, cols - 1))
        return there, device

    expected = jnp.int32(rows + cols - 2)
    for d in range(1, cols):
        greet((row, lax.rem(col + d, cols)))
    for d in range(1, rows):
        greet((lax.rem(row + d, rows), col))
    for k in (0, 2, 5, 7):
        there, device = neighbour(k)
        pl.when(there)(functools.partial(greet, device))
        expected = expected + jnp.where(there, 1, 0)
    for h in range(ratio):
        pl.when(jnp.logical_not(relays))(functools.partial(greet, (ratio * col + h, block)))
    expected = expected + jnp.where(relays, 0, ratio)


    i, j = iota((2 * LANES, LANES), 0), iota((2 * LANES, LANES), 1)
    edge = LANES - STEP
    lane = i % LANES
    goal = (i // LANES) * half_lanes + lane - j
    head = jnp.where(lane < STEP, goal, -LANES)
    tail = jnp.where(lane >= edge, goal - edge, -LANES)
    for phase in range(phases):
        pack_sel[phase] = one_hot(head == -phase * STEP)
        pack_sel[phases + phase] = one_hot(tail == -phase * STEP)

    def band(n, kernel_ref):
        span = (GROUP + 2) * chans
        c, k = iota((chans, span), 0), iota((chans, span), 1)
        for q in range(GROUP):
            for b in range(3):
                total = jnp.zeros((chans, span), F32)
                for a in range(3):
                    total += dot(kernel_ref[a, b], one_hot(k == c + (q + a) * chans))
                weights[n, b, pl.ds(q * chans, chans), :] = total.astype(BF16)

    pl.semaphore_wait(barrier, expected)

    def halo_copy(pad, n, k, own, base):
        dr, dc = WAYS[k]
        there, device = neighbour(k)
        if dc == 0:
            source = base if dr < 0 else base + depth - chans
            target = depth + chans if dr < 0 else 0
            src = own.at[:, pl.ds(source, chans)]
            dst = pad.at[:, pl.ds(target, chans)]
        else:
            mine, theirs = (0, 1) if dc < 0 else (1, 0)
            if dr == 0:
                src = packed.at[n, mine]
                dst = strips.at[n, theirs, pl.ds(0, fold_rows)]
            elif dr < 0:
                src = packed.at[n, mine, pl.ds(0, chans)]
                dst = strips.at[n, theirs, pl.ds(fold_rows + chans, chans)]
            else:
                src = packed.at[n, mine, pl.ds(fold_rows - chans, chans)]
                dst = strips.at[n, theirs, pl.ds(fold_rows, chans)]
        slot = n * 8 + k
        return there, remote(src, dst, halo_send.at[slot], halo_recv.at[slot], device)

    def halo_start(pad, n, own, base):
        for k in (1, 6):
            there, copy = halo_copy(pad, n, k, own, base)
            pl.when(there)(copy.start)
        for side, lane in ((0, 0), (1, width - LANES)):
            total = jnp.zeros((fold_rows, LANES), F32)
            for phase in range(phases):
                low = own[phase, pl.ds(base, fold_rows), pl.ds(lane, LANES)]
                high = own[phase, pl.ds(base + fold_rows, fold_rows), pl.ds(lane, LANES)]
                total += dot(
                    jnp.concatenate([low, high], axis=1), pack_sel[side * phases + phase]
                )
            packed[n, side] = total.astype(BF16)
            for k in (3, 0, 5) if side == 0 else (4, 2, 7):
                there, copy = halo_copy(pad, n, k, own, base)
                pl.when(there)(copy.start)

    def halo_finish(pad, n):
        for k in range(8):
            there, copy = halo_copy(pad, n, k, pad, chans)
            _, back = halo_copy(pad, n, 7 - k, pad, chans)

            @pl.when(there)
            def _(copy=copy, back=back):
                back.wait_recv()
                copy.wait_send()

    tiles = width // LANES

    def held(at):
        return jnp.concatenate([hidden[k, at, :] for k in range(tiles)], axis=1)

    def keep(at, values):
        for k in range(tiles):
            hidden[k, at, :] = values[:, k * LANES : (k + 1) * LANES]

    def fold(values):
        total = jnp.sum(values.reshape(-1, chans, width), axis=0)
        return sum(total[:, k : k + LANES] for k in range(0, width, LANES))

    def taps(pad, n, groups, acc):
        def body(phase, acc):
            for first, last in groups:
                low = first * GROUP * chans
                rows_in = ((last - first) * GROUP + 2) * chans
                middle = pad[phase, pl.ds(low, rows_in), :]
                blank = jnp.zeros((rows_in, STEP), BF16)
                shifted = (
                    jnp.concatenate([blank, middle[:, : width - STEP]], axis=1),
                    middle,
                    jnp.concatenate([middle[:, STEP:], blank], axis=1),
                )
                for g in range(last - first):
                    at = g * GROUP * chans
                    result = sum(
                        dot(weights[n, b], shifted[b][at : at + (GROUP + 2) * chans])
                        for b in range(3)
                    )
                    keep(pl.ds(phase * depth + low + at, GROUP * chans), result)
                    acc = acc + fold(result)
            return acc

        return lax.fori_loop(0, phases, body, acc, unroll=True)

    lanes = iota((GROUP * chans, LANES), 1)

    def strip_taps(n, side, acc):
        swap = lambda v: jnp.concatenate([v[:, half_lanes:], v[:, :half_lanes]], axis=1)
        whole = strips[n, side, pl.ds(0, fold_rows), :]
        up = strips[n, side, pl.ds(fold_rows, chans), :]
        down = strips[n, side, pl.ds(fold_rows + chans, chans), :]
        column = jnp.concatenate([swap(up), whole, swap(whole), down], axis=0)
        for g in range(count // GROUP):
            low = g * GROUP * chans
            added = dot(weights[n, 2 * side], column[low : low + (GROUP + 2) * chans])
            added = jnp.where(lanes < half_lanes, added, 0.0)
            edges[side, pl.ds(low, GROUP * chans), :] = added
            acc = acc + jnp.sum(added.reshape(GROUP, chans, LANES), axis=0)
        return acc

    def conv(pad, n):
        last = count // GROUP
        acc = taps(pad, n, ((1, last - 1),), jnp.zeros((chans, LANES), F32))
        halo_finish(pad, n)
        acc = taps(pad, n, ((0, 1), (last - 1, last)), acc)
        for side in range(2):
            acc = strip_taps(n, side, acc)
        return acc

    square = (chans, LANES)
    diagonal = iota(square, 0) == iota(square, 1)

    def to_lanes(values):
        return jnp.sum(jnp.where(diagonal, values, 0.0), axis=0, keepdims=True)

    def to_rows(values):
        spread = jnp.where(diagonal, jnp.broadcast_to(values, square), 0.0)
        return jnp.broadcast_to(jnp.sum(spread, axis=1, keepdims=True), square)

    def merge(own, other, size, stats, sends, recvs, n, axis_size, along_row):
        base = n * axis_size
        stats[base, pl.ds(0, 1), :] = own
        stats[base, pl.ds(1, 1), :] = other
        copies = []
        for d in range(1, axis_size):
            device = (
                (lax.rem(row + d, axis_size), col)
                if along_row
                else (row, lax.rem(col + d, axis_size))
            )
            copy = remote(
                stats.at[base],
                stats.at[base + d],
                sends.at[base + d],
                recvs.at[base + d],
                device,
            )
            copy.start()
            copies.append(copy)
        for copy in copies:
            copy.wait()
        means = [stats[base + d, pl.ds(0, 1), :] for d in range(axis_size)]
        mean = sum(means) / axis_size
        squares = sum(stats[base + d, pl.ds(1, 1), :] for d in range(axis_size))
        spread = sum((m - mean) * (m - mean) for m in means)
        return mean, squares + size * spread

    def norm(acc, n, gain, shift):
        own = jnp.broadcast_to(jnp.sum(acc, axis=1, keepdims=True) / cells, square)
        across = jnp.concatenate([own] * GROUP, axis=0)
        squares = jnp.zeros(square, F32)
        for phase in range(phases):
            for g in range(count // GROUP):
                low = g * GROUP * chans
                at = pl.ds(phase * depth + low, GROUP * chans)
                for k in range(tiles):
                    cell = hidden[k, at, :]
                    for side, tile, start in ((0, 0, 0), (1, tiles - 1, edge)):
                        if k == tile:
                            moved = pltpu.roll(
                                edges[side, pl.ds(low, GROUP * chans), :],
                                (start - phase * STEP) % LANES,
                                1,
                            )
                            wanted = lanes >= edge if side else lanes < STEP
                            cell = cell + jnp.where(wanted, moved, 0.0)
                            hidden[k, at, :] = cell
                    diff = cell - across
                    diff = (diff * diff).reshape(GROUP, chans, LANES)
                    squares = squares + jnp.sum(diff, axis=0)
        squares = jnp.broadcast_to(jnp.sum(squares, axis=1, keepdims=True), square)
        mean, squares = merge(
            to_lanes(own), to_lanes(squares), cells, col_stats, cs_send, cs_recv, n, cols, False
        )
        mean, squares = merge(
            mean, squares, cells * cols, row_stats, rs_send, rs_recv, n, rows, True
        )
        blank = jnp.zeros((1, LANES - chans), F32)
        gains = jnp.concatenate([gain[...], blank], axis=1)
        shifts = jnp.concatenate([shift[...], blank], axis=1)
        factor = gains * lax.rsqrt(squares / (cells * (rows * cols)) + EPSILON)
        repeat = lambda v: jnp.concatenate([to_rows(v)] * (width // LANES), axis=1)
        return repeat(mean), repeat(factor), repeat(shifts)

    halo_start(pad_one, 0, x_ref, 0)
    pad_one[:, pl.ds(chans, depth), :] = x_ref[...]
    band(0, first_ref)
    band(1, second_ref)
    mean, factor, shift = norm(conv(pad_one, 0), 0, gain_one, shift_one)

    def activate(phase, carry):
        for q in range(count):
            cell = held(pl.ds(phase * depth + q * chans, chans))
            cell = jnp.maximum((cell - mean) * factor + shift, 0.0)
            pad_two[phase, pl.ds((q + 1) * chans, chans), :] = cell.astype(BF16)
        return carry

    lax.fori_loop(0, phases, activate, 0, unroll=2)
    halo_start(pad_two, 1, pad_two, chans)
    mean, factor, shift = norm(conv(pad_two, 1), 1, gain_two, shift_two)

    def direct(source_col, source_block):
        z, p = lax.rem(source_col, 4), lax.rem(source_block, 4)
        chosen = (z == p) & (lax.rem(source_col + source_block, 8) < 4)
        for a, b in DIRECT:
            chosen = chosen | ((z == a) & (p == b))
        return chosen

    mine = direct(col, block)

    def crosses(target):
        return (2 * col < cols) != (2 * target < cols)

    def passes(d, k):
        target = lax.rem(col + d, cols)
        straight_on = direct(col, target)
        if k == pieces - 1:
            straight_on = straight_on | crosses(target) | (part == ratio - 1)
        return jnp.logical_not(straight_on)

    def span_of(k):
        p, at, size = table[k]
        return p, pl.ds(at, size)

    def source(h, k):
        return summed.at[(h, *span_of(k))]

    def landing(e, k):
        return got.at[(*span_of(k), pl.ds(e * count, count))]

    def waypoint(slot, k):
        return relay.at[(slot, *span_of(k))]

    def straight(h, k):
        return remote(
            source(h, k),
            landing(part, k),
            send.at[h * pieces + k],
            recv.at[part * pieces + k],
            (ratio * col + h, block),
        )

    def arrive(e, k):
        return remote(
            landing(e, k),
            landing(e, k),
            send.at[e * pieces + k],
            recv.at[e * pieces + k],
            (row, col),
        )

    def first_leg(h, k):
        slot = (lax.rem(block - col + cols, cols) - 1) * ratio + part
        return remote(
            source(h, k),
            waypoint(slot, k),
            send.at[h * pieces + k],
            relay_recv.at[slot * pieces + k],
            (ratio * col + h, col),
        )

    def second_leg(d, e, k):
        slot = (d - 1) * ratio + e
        return remote(
            waypoint(slot, k),
            landing(e, k),
            relay_send.at[slot * pieces + k],
            recv.at[e * pieces + k],
            (row, lax.rem(col + d, cols)),
        )

    def issue(k):
        for h in range(ratio):
            goes = relays | mine
            if k == pieces - 1:
                goes = goes | crosses(block) | (h == ratio - 1)
            here = relays & (part == h)

            @pl.when(goes & jnp.logical_not(here))
            def _(h=h):
                straight(h, k).start()

            @pl.when(jnp.logical_not(goes))
            def _(h=h):
                first_leg(h, k).start()

    def finish(phase, carry):
        for q in range(count):
            at = pl.ds(phase * depth + q * chans, chans)
            cell = (held(at) - mean) * factor + shift
            cell = (x_ref[phase, pl.ds(q * chans, chans), :].astype(F32) + cell).astype(BF16)
            for h in range(ratio):
                for p in range(parts):
                    summed[h, p, phase, q] = cell[
                        p * PART : (p + 1) * PART, h * height : (h + 1) * height
                    ]
            keep(at, cell.astype(F32))
        return carry

    for k in of_part(0):
        _, at, size = table[k]
        lax.fori_loop(at, at + size, finish, 0)
        issue(k)
    for k in range(len(of_part(0)), pieces):
        issue(k)

    @pl.when(relays)
    def _():
        for h in range(ratio):

            @pl.when(part == h)
            def _(h=h):
                got[:, :, pl.ds(h * count, count)] = summed[h]

    def forward(k):
        for d in range(1, cols):

            @pl.when(passes(d, k))
            def _(d=d):
                for e in range(ratio):
                    slot = (d - 1) * ratio + e
                    remote(
                        waypoint(slot, k),
                        waypoint(slot, k),
                        relay_send.at[slot * pieces + k],
                        relay_recv.at[slot * pieces + k],
                        (row, col),
                    ).wait_recv()
                    second_leg(d, e, k).start()

    def drain(k):
        for h in range(ratio):

            @pl.when(jnp.logical_not(relays & (part == h)))
            def _(h=h):
                straight(h, k).wait_send()

    span = ratio * depth
    unit = one_hot(iota((height, height), 0) == iota((height, height), 1))
    for p in range(parts):

        @pl.when(relays)
        def _(p=p):
            for k in of_part(p):
                forward(k)

        if p > 0:
            for k in of_part(p - 1):
                drain(k)

        def collect(phase, carry, p=p):
            for q in range(ratio * count):
                wide[pl.ds(phase * span + q * chans + p * PART, PART), :] = got[
                    p, phase, q
                ].astype(F32)
            return carry

        for k in of_part(p):
            for e in range(ratio):

                @pl.when(jnp.logical_not(relays & (part == e)))
                def _(e=e, k=k):
                    arrive(e, k).wait_recv()

            _, at, size = table[k]
            lax.fori_loop(at, at + size, collect, 0)

        def turn(c, carry):
            own = jnp.concatenate(
                [
                    held(pl.ds(q * chans + c, phases, stride=depth))
                    for q in range(count)
                ],
                axis=0,
            )
            other = jnp.concatenate(
                [
                    wide[pl.ds(q * chans + c, phases, stride=span), :]
                    for q in range(ratio * count)
                ],
                axis=0,
            )
            total = own + lax.dot_general(
                unit, other.astype(BF16), (((1,), (1,)), ((), ())), preferred_element_type=F32
            )
            out_ref[c] = (total * 0.5).astype(BF16)
            return carry

        lax.fori_loop(p * PART, (p + 1) * PART, turn, 0, unroll=4)

    for k in of_part(parts - 1):
        drain(k)

    @pl.when(relays)
    def _():
        for k in range(pieces):
            for d in range(1, cols):

                @pl.when(passes(d, k))
                def _(d=d, k=k):
                    for e in range(ratio):
                        second_leg(d, e, k).wait_send()


def run(rows, cols, features, first, second, scales):
    chans, height, width = features.shape
    count = height // STEP
    depth = count * chans
    ratio = rows // cols
    slots = (cols - 1) * ratio
    parts = chans // PART
    pieces = len(piece_table(parts))
    full = depth + 2 * chans
    x = jnp.transpose(features.reshape(chans, count, STEP, width), (2, 1, 0, 3))
    x = x.reshape(STEP, depth, width)
    scales = [v.reshape(1, chans) for v in scales]
    vmem = pl.BlockSpec(memory_space=pltpu.VMEM)
    dma = pltpu.SemaphoreType.DMA
    return pl.pallas_call(
        functools.partial(kernel, rows, cols),
        out_shape=jax.ShapeDtypeStruct(features.shape, BF16),
        in_specs=[vmem] * 7,
        out_specs=vmem,
        scratch_shapes=[
            pltpu.VMEM((STEP, full, width), BF16),
            pltpu.VMEM((STEP, full, width), BF16),
            pltpu.VMEM((width // LANES, STEP * depth, LANES), F32),
            pltpu.VMEM((2 * STEP, 2 * LANES, LANES), BF16),
            pltpu.VMEM((2, depth, LANES), F32),
            pltpu.VMEM((2, 3, GROUP * chans, (GROUP + 2) * chans), BF16),
            pltpu.VMEM((2, 2, depth // 2, LANES), BF16),
            pltpu.VMEM((2, 2, depth // 2 + 2 * chans, LANES), BF16),
            pltpu.VMEM((2 * cols, 2, LANES), F32),
            pltpu.VMEM((2 * rows, 2, LANES), F32),
            pltpu.VMEM((ratio, parts, STEP, count, PART, height), BF16),
            pltpu.VMEM((parts, STEP, ratio * count, PART, height), BF16),
            pltpu.VMEM((STEP * ratio * depth, height), F32),
            pltpu.VMEM((slots, parts, STEP, count, PART, height), BF16),
            dma((16,)),
            dma((16,)),
            dma((2 * cols,)),
            dma((2 * cols,)),
            dma((2 * rows,)),
            dma((2 * rows,)),
            dma((ratio * pieces,)),
            dma((ratio * pieces,)),
            dma((slots * pieces,)),
            dma((slots * pieces,)),
        ],
        compiler_params=pltpu.CompilerParams(
            collective_id=0, has_side_effects=True, vmem_limit_bytes=44 * 1024 * 1024
        ),
    )(x, first, second, *scales)


def solution(mesh):
    rows, cols = mesh.shape["row"], mesh.shape["col"]

    def per_device(features, first, second, gain_one, shift_one, gain_two, shift_two):
        scales = (gain_one, shift_one, gain_two, shift_two)
        return run(rows, cols, features, first, second, scales)

    placed = (P(None, "row", "col"), P(), P(), P(), P(), P(), P())
    return jax.shard_map(
        per_device, mesh=mesh, in_specs=placed, out_specs=P(None, "row", "col"), check_vma=False
    )
```

```python
import functools

import jax
import jax.numpy as jnp
from jax import lax
from jax.experimental import pallas as pl
from jax.experimental.pallas import tpu as pltpu
from jax.sharding import PartitionSpec as P

STEP = 8
GROUP = 4
EPSILON = 1e-05
LANES = 128
PART = 16
MESH = pl.DeviceIdType.MESH
BF16 = jnp.bfloat16
F32 = jnp.float32

DIRECT = ((0, 1), (0, 2), (1, 3), (2, 0), (3, 1), (3, 2))

WAYS = ((-1, -1), (-1, 0), (-1, 1), (0, -1), (0, 1), (1, -1), (1, 0), (1, 1))


def iota(shape, dim):
    return lax.broadcasted_iota(jnp.int32, shape, dim)


def one_hot(mask):
    return jnp.where(mask, 1.0, 0.0).astype(BF16)


def dot(a, b):
    return jnp.dot(a, b, preferred_element_type=F32)


def piece_table(parts):
    table = []
    for p in range(parts):
        sizes = (1, 1, 2, 2, 2) if p < parts - 1 else (2, 2, 2, 1, 1)
        at = 0
        for size in sizes:
            table.append((p, at, size))
            at += size
    return table


def remote(src, dst, send, recv, device):
    return pltpu.make_async_remote_copy(
        src_ref=src,
        dst_ref=dst,
        send_sem=send,
        recv_sem=recv,
        device_id=device,
        device_id_type=MESH,
    )


def kernel(
    rows,
    cols,
    x_ref,
    first_ref,
    second_ref,
    gain_one,
    shift_one,
    gain_two,
    shift_two,
    out_ref,
    pad_one,
    pad_two,
    hidden,
    pack_sel,
    edges,
    weights,
    packed,
    strips,
    col_stats,
    row_stats,
    summed,
    got,
    wide,
    relay,
    halo_send,
    halo_recv,
    cs_send,
    cs_recv,
    rs_send,
    rs_recv,
    send,
    recv,
    relay_send,
    relay_recv,
):
    row = lax.axis_index("row")
    col = lax.axis_index("col")
    phases, depth, width = x_ref.shape
    chans, height, _ = out_ref.shape
    count = depth // chans
    full = depth + 2 * chans
    fold_rows = depth // 2
    half_lanes = LANES // 2
    cells = float(phases * count * width)
    ratio = rows // cols
    block = lax.div(row, ratio)
    part = lax.rem(row, ratio)
    relays = block == col
    parts = chans // PART
    table = piece_table(parts)
    pieces = len(table)
    of_part = lambda p: [k for k in range(pieces) if table[k][0] == p]

    for pad in (pad_one, pad_two):
        for at, size in ((0, chans), (depth + chans, chans)):
            pad[:, pl.ds(at, size), :] = jnp.zeros((phases, size, width), BF16)
    strips[...] = jnp.zeros_like(strips)

    barrier = pltpu.get_barrier_semaphore()

    def greet(device):
        pl.semaphore_signal(barrier, inc=1, device_id=device, device_id_type=MESH)

    def neighbour(k):
        dr, dc = WAYS[k]
        there = jnp.bool_(True)
        if dr:
            there = there & ((row > 0) if dr < 0 else (row < rows - 1))
        if dc:
            there = there & ((col > 0) if dc < 0 else (col < cols - 1))
        device = (jnp.clip(row + dr, 0, rows - 1), jnp.clip(col + dc, 0, cols - 1))
        return there, device

    expected = jnp.int32(rows + cols - 2)
    for d in range(1, cols):
        greet((row, lax.rem(col + d, cols)))
    for d in range(1, rows):
        greet((lax.rem(row + d, rows), col))
    for k in (0, 2, 5, 7):
        there, device = neighbour(k)
        pl.when(there)(functools.partial(greet, device))
        expected = expected + jnp.where(there, 1, 0)
    for h in range(ratio):
        pl.when(jnp.logical_not(relays))(functools.partial(greet, (ratio * col + h, block)))
    expected = expected + jnp.where(relays, 0, ratio)


    i, j = iota((2 * LANES, LANES), 0), iota((2 * LANES, LANES), 1)
    edge = LANES - STEP
    lane = i % LANES
    goal = (i // LANES) * half_lanes + lane - j
    head = jnp.where(lane < STEP, goal, -LANES)
    tail = jnp.where(lane >= edge, goal - edge, -LANES)
    for phase in range(phases):
        pack_sel[phase] = one_hot(head == -phase * STEP)
        pack_sel[phases + phase] = one_hot(tail == -phase * STEP)

    def band(n, kernel_ref):
        span = (GROUP + 2) * chans
        c, k = iota((chans, span), 0), iota((chans, span), 1)
        for q in range(GROUP):
            for b in range(3):
                total = jnp.zeros((chans, span), F32)
                for a in range(3):
                    total += dot(kernel_ref[a, b], one_hot(k == c + (q + a) * chans))
                weights[n, b, pl.ds(q * chans, chans), :] = total.astype(BF16)

    pl.semaphore_wait(barrier, expected)

    def halo_copy(pad, n, k, own, base):
        dr, dc = WAYS[k]
        there, device = neighbour(k)
        if dc == 0:
            source = base if dr < 0 else base + depth - chans
            target = depth + chans if dr < 0 else 0
            src = own.at[:, pl.ds(source, chans)]
            dst = pad.at[:, pl.ds(target, chans)]
        else:
            mine, theirs = (0, 1) if dc < 0 else (1, 0)
            if dr == 0:
                src = packed.at[n, mine]
                dst = strips.at[n, theirs, pl.ds(0, fold_rows)]
            elif dr < 0:
                src = packed.at[n, mine, pl.ds(0, chans)]
                dst = strips.at[n, theirs, pl.ds(fold_rows + chans, chans)]
            else:
                src = packed.at[n, mine, pl.ds(fold_rows - chans, chans)]
                dst = strips.at[n, theirs, pl.ds(fold_rows, chans)]
        slot = n * 8 + k
        return there, remote(src, dst, halo_send.at[slot], halo_recv.at[slot], device)

    def halo_start(pad, n, own, base):
        for k in (1, 6):
            there, copy = halo_copy(pad, n, k, own, base)
            pl.when(there)(copy.start)
        for side, lane in ((0, 0), (1, width - LANES)):
            total = jnp.zeros((fold_rows, LANES), F32)
            for phase in range(phases):
                low = own[phase, pl.ds(base, fold_rows), pl.ds(lane, LANES)]
                high = own[phase, pl.ds(base + fold_rows, fold_rows), pl.ds(lane, LANES)]
                total += dot(
                    jnp.concatenate([low, high], axis=1), pack_sel[side * phases + phase]
                )
            packed[n, side] = total.astype(BF16)
            for k in (3, 0, 5) if side == 0 else (4, 2, 7):
                there, copy = halo_copy(pad, n, k, own, base)
                pl.when(there)(copy.start)

    def halo_finish(pad, n):
        for k in range(8):
            there, copy = halo_copy(pad, n, k, pad, chans)
            _, back = halo_copy(pad, n, 7 - k, pad, chans)

            @pl.when(there)
            def _(copy=copy, back=back):
                back.wait_recv()
                copy.wait_send()

    tiles = width // LANES

    def held(at):
        return jnp.concatenate([hidden[k, at, :] for k in range(tiles)], axis=1)

    def keep(at, values):
        for k in range(tiles):
            hidden[k, at, :] = values[:, k * LANES : (k + 1) * LANES]

    def fold(values):
        total = jnp.sum(values.reshape(-1, chans, width), axis=0)
        return sum(total[:, k : k + LANES] for k in range(0, width, LANES))

    def taps(pad, n, groups, acc):
        def body(phase, acc):
            for first, last in groups:
                low = first * GROUP * chans
                rows_in = ((last - first) * GROUP + 2) * chans
                middle = pad[phase, pl.ds(low, rows_in), :]
                blank = jnp.zeros((rows_in, STEP), BF16)
                shifted = (
                    jnp.concatenate([blank, middle[:, : width - STEP]], axis=1),
                    middle,
                    jnp.concatenate([middle[:, STEP:], blank], axis=1),
                )
                for g in range(last - first):
                    at = g * GROUP * chans
                    result = sum(
                        dot(weights[n, b], shifted[b][at : at + (GROUP + 2) * chans])
                        for b in range(3)
                    )
                    keep(pl.ds(phase * depth + low + at, GROUP * chans), result)
                    acc = acc + fold(result)
            return acc

        return lax.fori_loop(0, phases, body, acc, unroll=True)

    lanes = iota((GROUP * chans, LANES), 1)

    def strip_taps(n, side, acc):
        swap = lambda v: jnp.concatenate([v[:, half_lanes:], v[:, :half_lanes]], axis=1)
        whole = strips[n, side, pl.ds(0, fold_rows), :]
        up = strips[n, side, pl.ds(fold_rows, chans), :]
        down = strips[n, side, pl.ds(fold_rows + chans, chans), :]
        column = jnp.concatenate([swap(up), whole, swap(whole), down], axis=0)
        for g in range(count // GROUP):
            low = g * GROUP * chans
            added = dot(weights[n, 2 * side], column[low : low + (GROUP + 2) * chans])
            added = jnp.where(lanes < half_lanes, added, 0.0)
            edges[side, pl.ds(low, GROUP * chans), :] = added
            acc = acc + jnp.sum(added.reshape(GROUP, chans, LANES), axis=0)
        return acc

    def conv(pad, n):
        last = count // GROUP
        acc = taps(pad, n, ((1, last - 1),), jnp.zeros((chans, LANES), F32))
        halo_finish(pad, n)
        acc = taps(pad, n, ((0, 1), (last - 1, last)), acc)
        for side in range(2):
            acc = strip_taps(n, side, acc)
        return acc

    square = (chans, LANES)
    diagonal = iota(square, 0) == iota(square, 1)

    def to_lanes(values):
        return jnp.sum(jnp.where(diagonal, values, 0.0), axis=0, keepdims=True)

    def to_rows(values):
        spread = jnp.where(diagonal, jnp.broadcast_to(values, square), 0.0)
        return jnp.broadcast_to(jnp.sum(spread, axis=1, keepdims=True), square)

    def merge(own, other, size, stats, sends, recvs, n, axis_size, along_row):
        base = n * axis_size
        stats[base, pl.ds(0, 1), :] = own
        stats[base, pl.ds(1, 1), :] = other
        copies = []
        for d in range(1, axis_size):
            device = (
                (lax.rem(row + d, axis_size), col)
                if along_row
                else (row, lax.rem(col + d, axis_size))
            )
            copy = remote(
                stats.at[base],
                stats.at[base + d],
                sends.at[base + d],
                recvs.at[base + d],
                device,
            )
            copy.start()
            copies.append(copy)
        if n == 0 and not along_row:
            band(1, second_ref)
        for copy in copies:
            copy.wait()
        means = [stats[base + d, pl.ds(0, 1), :] for d in range(axis_size)]
        mean = sum(means) / axis_size
        squares = sum(stats[base + d, pl.ds(1, 1), :] for d in range(axis_size))
        spread = sum((m - mean) * (m - mean) for m in means)
        return mean, squares + size * spread

    def norm(acc, n, gain, shift):
        own = jnp.broadcast_to(jnp.sum(acc, axis=1, keepdims=True) / cells, square)
        across = jnp.concatenate([own] * GROUP, axis=0)
        squares = jnp.zeros(square, F32)
        for phase in range(phases):
            for g in range(count // GROUP):
                low = g * GROUP * chans
                at = pl.ds(phase * depth + low, GROUP * chans)
                for k in range(tiles):
                    cell = hidden[k, at, :]
                    for side, tile, start in ((0, 0, 0), (1, tiles - 1, edge)):
                        if k == tile:
                            moved = pltpu.roll(
                                edges[side, pl.ds(low, GROUP * chans), :],
                                (start - phase * STEP) % LANES,
                                1,
                            )
                            wanted = lanes >= edge if side else lanes < STEP
                            cell = cell + jnp.where(wanted, moved, 0.0)
                            hidden[k, at, :] = cell
                    diff = cell - across
                    diff = (diff * diff).reshape(GROUP, chans, LANES)
                    squares = squares + jnp.sum(diff, axis=0)
        squares = jnp.broadcast_to(jnp.sum(squares, axis=1, keepdims=True), square)
        mean, squares = merge(
            to_lanes(own), to_lanes(squares), cells, col_stats, cs_send, cs_recv, n, cols, False
        )
        mean, squares = merge(
            mean, squares, cells * cols, row_stats, rs_send, rs_recv, n, rows, True
        )
        blank = jnp.zeros((1, LANES - chans), F32)
        gains = jnp.concatenate([gain[...], blank], axis=1)
        shifts = jnp.concatenate([shift[...], blank], axis=1)
        factor = gains * lax.rsqrt(squares / (cells * (rows * cols)) + EPSILON)
        repeat = lambda v: jnp.concatenate([to_rows(v)] * (width // LANES), axis=1)
        return repeat(mean), repeat(factor), repeat(shifts)

    halo_start(pad_one, 0, x_ref, 0)
    pad_one[:, pl.ds(chans, depth), :] = x_ref[...]
    band(0, first_ref)
    mean, factor, shift = norm(conv(pad_one, 0), 0, gain_one, shift_one)

    def activate(phase, carry):
        for q in range(count):
            cell = held(pl.ds(phase * depth + q * chans, chans))
            cell = jnp.maximum((cell - mean) * factor + shift, 0.0)
            pad_two[phase, pl.ds((q + 1) * chans, chans), :] = cell.astype(BF16)
        return carry

    lax.fori_loop(0, phases, activate, 0, unroll=2)
    halo_start(pad_two, 1, pad_two, chans)
    mean, factor, shift = norm(conv(pad_two, 1), 1, gain_two, shift_two)

    def direct(source_col, source_block):
        z, p = lax.rem(source_col, 4), lax.rem(source_block, 4)
        chosen = (z == p) & (lax.rem(source_col + source_block, 8) < 4)
        for a, b in DIRECT:
            chosen = chosen | ((z == a) & (p == b))
        return chosen

    mine = direct(col, block)

    def crosses(target):
        return (2 * col < cols) != (2 * target < cols)

    def passes(d, k):
        target = lax.rem(col + d, cols)
        straight_on = direct(col, target)
        if k == pieces - 1:
            straight_on = straight_on | crosses(target) | (part == ratio - 1)
        return jnp.logical_not(straight_on)

    def span_of(k):
        p, at, size = table[k]
        return p, pl.ds(at, size)

    def source(h, k):
        return summed.at[(h, *span_of(k))]

    def landing(e, k):
        return got.at[(*span_of(k), pl.ds(e * count, count))]

    def waypoint(slot, k):
        return relay.at[(slot, *span_of(k))]

    def straight(h, k):
        return remote(
            source(h, k),
            landing(part, k),
            send.at[h * pieces + k],
            recv.at[part * pieces + k],
            (ratio * col + h, block),
        )

    def arrive(e, k):
        return remote(
            landing(e, k),
            landing(e, k),
            send.at[e * pieces + k],
            recv.at[e * pieces + k],
            (row, col),
        )

    def first_leg(h, k):
        slot = (lax.rem(block - col + cols, cols) - 1) * ratio + part
        return remote(
            source(h, k),
            waypoint(slot, k),
            send.at[h * pieces + k],
            relay_recv.at[slot * pieces + k],
            (ratio * col + h, col),
        )

    def second_leg(d, e, k):
        slot = (d - 1) * ratio + e
        return remote(
            waypoint(slot, k),
            landing(e, k),
            relay_send.at[slot * pieces + k],
            recv.at[e * pieces + k],
            (row, lax.rem(col + d, cols)),
        )

    def issue(k):
        for h in range(ratio):
            goes = relays | mine
            if k == pieces - 1:
                goes = goes | crosses(block) | (h == ratio - 1)
            here = relays & (part == h)

            @pl.when(goes & jnp.logical_not(here))
            def _(h=h):
                straight(h, k).start()

            @pl.when(jnp.logical_not(goes))
            def _(h=h):
                first_leg(h, k).start()

    def finish(phase, carry):
        for q in range(count):
            at = pl.ds(phase * depth + q * chans, chans)
            cell = (held(at) - mean) * factor + shift
            cell = (x_ref[phase, pl.ds(q * chans, chans), :].astype(F32) + cell).astype(BF16)
            for h in range(ratio):
                for p in range(parts):
                    summed[h, p, phase, q] = cell[
                        p * PART : (p + 1) * PART, h * height : (h + 1) * height
                    ]
            keep(at, cell.astype(F32))
        return carry

    for k in of_part(0):
        _, at, size = table[k]
        lax.fori_loop(at, at + size, finish, 0)
        issue(k)
    for k in range(len(of_part(0)), pieces):
        issue(k)

    @pl.when(relays)
    def _():
        for h in range(ratio):

            @pl.when(part == h)
            def _(h=h):
                got[:, :, pl.ds(h * count, count)] = summed[h]

    def forward(k):
        for d in range(1, cols):

            @pl.when(passes(d, k))
            def _(d=d):
                for e in range(ratio):
                    slot = (d - 1) * ratio + e
                    remote(
                        waypoint(slot, k),
                        waypoint(slot, k),
                        relay_send.at[slot * pieces + k],
                        relay_recv.at[slot * pieces + k],
                        (row, col),
                    ).wait_recv()
                    second_leg(d, e, k).start()

    def drain(k):
        for h in range(ratio):

            @pl.when(jnp.logical_not(relays & (part == h)))
            def _(h=h):
                straight(h, k).wait_send()

    span = ratio * depth
    unit = one_hot(iota((height, height), 0) == iota((height, height), 1))
    for p in range(parts):

        @pl.when(relays)
        def _(p=p):
            for k in of_part(p):
                forward(k)

        if p > 0:
            for k in of_part(p - 1):
                drain(k)

        def collect(phase, carry, p=p):
            for q in range(ratio * count):
                wide[pl.ds(phase * span + q * chans + p * PART, PART), :] = got[
                    p, phase, q
                ].astype(F32)
            return carry

        for k in of_part(p):
            for e in range(ratio):

                @pl.when(jnp.logical_not(relays & (part == e)))
                def _(e=e, k=k):
                    arrive(e, k).wait_recv()

            _, at, size = table[k]
            lax.fori_loop(at, at + size, collect, 0)

        def turn(c, carry):
            own = jnp.concatenate(
                [
                    held(pl.ds(q * chans + c, phases, stride=depth))
                    for q in range(count)
                ],
                axis=0,
            )
            other = jnp.concatenate(
                [
                    wide[pl.ds(q * chans + c, phases, stride=span), :]
                    for q in range(ratio * count)
                ],
                axis=0,
            )
            total = own + lax.dot_general(
                unit, other.astype(BF16), (((1,), (1,)), ((), ())), preferred_element_type=F32
            )
            out_ref[c] = (total * 0.5).astype(BF16)
            return carry

        lax.fori_loop(p * PART, (p + 1) * PART, turn, 0, unroll=4)

    for k in of_part(parts - 1):
        drain(k)

    @pl.when(relays)
    def _():
        for k in range(pieces):
            for d in range(1, cols):

                @pl.when(passes(d, k))
                def _(d=d, k=k):
                    for e in range(ratio):
                        second_leg(d, e, k).wait_send()


def run(rows, cols, features, first, second, scales):
    chans, height, width = features.shape
    count = height // STEP
    depth = count * chans
    ratio = rows // cols
    slots = (cols - 1) * ratio
    parts = chans // PART
    pieces = len(piece_table(parts))
    full = depth + 2 * chans
    x = jnp.transpose(features.reshape(chans, count, STEP, width), (2, 1, 0, 3))
    x = x.reshape(STEP, depth, width)
    scales = [v.reshape(1, chans) for v in scales]
    vmem = pl.BlockSpec(memory_space=pltpu.VMEM)
    dma = pltpu.SemaphoreType.DMA
    return pl.pallas_call(
        functools.partial(kernel, rows, cols),
        out_shape=jax.ShapeDtypeStruct(features.shape, BF16),
        in_specs=[vmem] * 7,
        out_specs=vmem,
        scratch_shapes=[
            pltpu.VMEM((STEP, full, width), BF16),
            pltpu.VMEM((STEP, full, width), BF16),
            pltpu.VMEM((width // LANES, STEP * depth, LANES), F32),
            pltpu.VMEM((2 * STEP, 2 * LANES, LANES), BF16),
            pltpu.VMEM((2, depth, LANES), F32),
            pltpu.VMEM((2, 3, GROUP * chans, (GROUP + 2) * chans), BF16),
            pltpu.VMEM((2, 2, depth // 2, LANES), BF16),
            pltpu.VMEM((2, 2, depth // 2 + 2 * chans, LANES), BF16),
            pltpu.VMEM((2 * cols, 2, LANES), F32),
            pltpu.VMEM((2 * rows, 2, LANES), F32),
            pltpu.VMEM((ratio, parts, STEP, count, PART, height), BF16),
            pltpu.VMEM((parts, STEP, ratio * count, PART, height), BF16),
            pltpu.VMEM((STEP * ratio * depth, height), F32),
            pltpu.VMEM((slots, parts, STEP, count, PART, height), BF16),
            dma((16,)),
            dma((16,)),
            dma((2 * cols,)),
            dma((2 * cols,)),
            dma((2 * rows,)),
            dma((2 * rows,)),
            dma((ratio * pieces,)),
            dma((ratio * pieces,)),
            dma((slots * pieces,)),
            dma((slots * pieces,)),
        ],
        compiler_params=pltpu.CompilerParams(
            collective_id=0, has_side_effects=True, vmem_limit_bytes=44 * 1024 * 1024
        ),
    )(x, first, second, *scales)


def solution(mesh):
    rows, cols = mesh.shape["row"], mesh.shape["col"]

    def per_device(features, first, second, gain_one, shift_one, gain_two, shift_two):
        scales = (gain_one, shift_one, gain_two, shift_two)
        return run(rows, cols, features, first, second, scales)

    placed = (P(None, "row", "col"), P(), P(), P(), P(), P(), P())
    return jax.shard_map(
        per_device, mesh=mesh, in_specs=placed, out_specs=P(None, "row", "col"), check_vma=False
    )
```

```python
import functools

import jax
import jax.numpy as jnp
from jax import lax
from jax.experimental import pallas as pl
from jax.experimental.pallas import tpu as pltpu
from jax.sharding import PartitionSpec as P

STEP = 8
GROUP = 4
EPSILON = 1e-05
LANES = 128
PART = 16
MESH = pl.DeviceIdType.MESH
BF16 = jnp.bfloat16
F32 = jnp.float32

DIRECT = ((0, 1), (0, 2), (1, 3), (2, 0), (3, 1), (3, 2))

WAYS = ((-1, -1), (-1, 0), (-1, 1), (0, -1), (0, 1), (1, -1), (1, 0), (1, 1))


def iota(shape, dim):
    return lax.broadcasted_iota(jnp.int32, shape, dim)


def one_hot(mask):
    return jnp.where(mask, 1.0, 0.0).astype(BF16)


def dot(a, b):
    return jnp.dot(a, b, preferred_element_type=F32)


def piece_table(parts):
    table = []
    for p in range(parts):
        sizes = (1, 1, 2, 2, 2) if p < parts - 1 else (2, 2, 2, 1, 1)
        at = 0
        for size in sizes:
            table.append((p, at, size))
            at += size
    return table


def remote(src, dst, send, recv, device):
    return pltpu.make_async_remote_copy(
        src_ref=src,
        dst_ref=dst,
        send_sem=send,
        recv_sem=recv,
        device_id=device,
        device_id_type=MESH,
    )


def kernel(
    rows,
    cols,
    x_ref,
    first_ref,
    second_ref,
    gain_one,
    shift_one,
    gain_two,
    shift_two,
    out_ref,
    pad_one,
    pad_two,
    hidden,
    pack_sel,
    edges,
    weights,
    packed,
    strips,
    col_stats,
    row_stats,
    summed,
    got,
    wide,
    relay,
    halo_send,
    halo_recv,
    cs_send,
    cs_recv,
    rs_send,
    rs_recv,
    send,
    recv,
    relay_send,
    relay_recv,
):
    row = lax.axis_index("row")
    col = lax.axis_index("col")
    phases, depth, width = x_ref.shape
    chans, height, _ = out_ref.shape
    count = depth // chans
    full = depth + 2 * chans
    fold_rows = depth // 2
    half_lanes = LANES // 2
    cells = float(phases * count * width)
    ratio = rows // cols
    block = lax.div(row, ratio)
    part = lax.rem(row, ratio)
    relays = block == col
    parts = chans // PART
    table = piece_table(parts)
    pieces = len(table)
    of_part = lambda p: [k for k in range(pieces) if table[k][0] == p]

    for pad in (pad_one, pad_two):
        for at, size in ((0, chans), (depth + chans, chans)):
            pad[:, pl.ds(at, size), :] = jnp.zeros((phases, size, width), BF16)
    strips[...] = jnp.zeros_like(strips)

    barrier = pltpu.get_barrier_semaphore()

    def greet(device):
        pl.semaphore_signal(barrier, inc=1, device_id=device, device_id_type=MESH)

    def neighbour(k):
        dr, dc = WAYS[k]
        there = jnp.bool_(True)
        if dr:
            there = there & ((row > 0) if dr < 0 else (row < rows - 1))
        if dc:
            there = there & ((col > 0) if dc < 0 else (col < cols - 1))
        device = (jnp.clip(row + dr, 0, rows - 1), jnp.clip(col + dc, 0, cols - 1))
        return there, device

    expected = jnp.int32(rows + cols - 2)
    for d in range(1, cols):
        greet((row, lax.rem(col + d, cols)))
    for d in range(1, rows):
        greet((lax.rem(row + d, rows), col))
    for k in (0, 2, 5, 7):
        there, device = neighbour(k)
        pl.when(there)(functools.partial(greet, device))
        expected = expected + jnp.where(there, 1, 0)
    for h in range(ratio):
        pl.when(jnp.logical_not(relays))(functools.partial(greet, (ratio * col + h, block)))
    expected = expected + jnp.where(relays, 0, ratio)


    i, j = iota((2 * LANES, LANES), 0), iota((2 * LANES, LANES), 1)
    edge = LANES - STEP
    lane = i % LANES
    goal = (i // LANES) * half_lanes + lane - j
    head = jnp.where(lane < STEP, goal, -LANES)
    tail = jnp.where(lane >= edge, goal - edge, -LANES)
    for phase in range(phases):
        pack_sel[phase] = one_hot(head == -phase * STEP)
        pack_sel[phases + phase] = one_hot(tail == -phase * STEP)

    def band(n, kernel_ref):
        span = (GROUP + 2) * chans
        c, k = iota((chans, span), 0), iota((chans, span), 1)
        for q in range(GROUP):
            for b in range(3):
                total = jnp.zeros((chans, span), F32)
                for a in range(3):
                    total += dot(kernel_ref[a, b], one_hot(k == c + (q + a) * chans))
                weights[n, b, pl.ds(q * chans, chans), :] = total.astype(BF16)

    pl.semaphore_wait(barrier, expected)

    def halo_copy(pad, n, k, own, base):
        dr, dc = WAYS[k]
        there, device = neighbour(k)
        if dc == 0:
            source = base if dr < 0 else base + depth - chans
            target = depth + chans if dr < 0 else 0
            src = own.at[:, pl.ds(source, chans)]
            dst = pad.at[:, pl.ds(target, chans)]
        else:
            mine, theirs = (0, 1) if dc < 0 else (1, 0)
            if dr == 0:
                src = packed.at[n, mine]
                dst = strips.at[n, theirs, pl.ds(0, fold_rows)]
            elif dr < 0:
                src = packed.at[n, mine, pl.ds(0, chans)]
                dst = strips.at[n, theirs, pl.ds(fold_rows + chans, chans)]
            else:
                src = packed.at[n, mine, pl.ds(fold_rows - chans, chans)]
                dst = strips.at[n, theirs, pl.ds(fold_rows, chans)]
        slot = n * 8 + k
        return there, remote(src, dst, halo_send.at[slot], halo_recv.at[slot], device)

    def halo_start(pad, n, own, base):
        for k in (1, 6):
            there, copy = halo_copy(pad, n, k, own, base)
            pl.when(there)(copy.start)
        for side, lane in ((0, 0), (1, width - LANES)):
            total = jnp.zeros((fold_rows, LANES), F32)
            for phase in range(phases):
                low = own[phase, pl.ds(base, fold_rows), pl.ds(lane, LANES)]
                high = own[phase, pl.ds(base + fold_rows, fold_rows), pl.ds(lane, LANES)]
                total += dot(
                    jnp.concatenate([low, high], axis=1), pack_sel[side * phases + phase]
                )
            packed[n, side] = total.astype(BF16)
            for k in (3, 0, 5) if side == 0 else (4, 2, 7):
                there, copy = halo_copy(pad, n, k, own, base)
                pl.when(there)(copy.start)

    def halo_finish(pad, n):
        for k in range(8):
            there, copy = halo_copy(pad, n, k, pad, chans)
            _, back = halo_copy(pad, n, 7 - k, pad, chans)

            @pl.when(there)
            def _(copy=copy, back=back):
                back.wait_recv()
                copy.wait_send()

    tiles = width // LANES

    def held(at):
        return jnp.concatenate([hidden[k, at, :] for k in range(tiles)], axis=1)

    def keep(at, values):
        for k in range(tiles):
            hidden[k, at, :] = values[:, k * LANES : (k + 1) * LANES]

    def fold(values):
        total = jnp.sum(values.reshape(-1, chans, width), axis=0)
        return sum(total[:, k : k + LANES] for k in range(0, width, LANES))

    def taps(pad, n, groups, acc):
        def body(phase, acc):
            for first, last in groups:
                low = first * GROUP * chans
                rows_in = ((last - first) * GROUP + 2) * chans
                middle = pad[phase, pl.ds(low, rows_in), :]
                blank = jnp.zeros((rows_in, STEP), BF16)
                shifted = (
                    jnp.concatenate([blank, middle[:, : width - STEP]], axis=1),
                    middle,
                    jnp.concatenate([middle[:, STEP:], blank], axis=1),
                )
                for g in range(last - first):
                    at = g * GROUP * chans
                    result = sum(
                        dot(weights[n, b], shifted[b][at : at + (GROUP + 2) * chans])
                        for b in range(3)
                    )
                    keep(pl.ds(phase * depth + low + at, GROUP * chans), result)
                    acc = acc + fold(result)
            return acc

        return lax.fori_loop(0, phases, body, acc, unroll=True)

    lanes = iota((GROUP * chans, LANES), 1)

    def strip_taps(n, side, acc):
        swap = lambda v: jnp.concatenate([v[:, half_lanes:], v[:, :half_lanes]], axis=1)
        whole = strips[n, side, pl.ds(0, fold_rows), :]
        up = strips[n, side, pl.ds(fold_rows, chans), :]
        down = strips[n, side, pl.ds(fold_rows + chans, chans), :]
        column = jnp.concatenate([swap(up), whole, swap(whole), down], axis=0)
        for g in range(count // GROUP):
            low = g * GROUP * chans
            added = dot(weights[n, 2 * side], column[low : low + (GROUP + 2) * chans])
            added = jnp.where(lanes < half_lanes, added, 0.0)
            edges[side, pl.ds(low, GROUP * chans), :] = added
            acc = acc + jnp.sum(added.reshape(GROUP, chans, LANES), axis=0)
        return acc

    def conv(pad, n):
        last = count // GROUP
        acc = taps(pad, n, ((1, last - 1),), jnp.zeros((chans, LANES), F32))
        halo_finish(pad, n)
        acc = taps(pad, n, ((0, 1), (last - 1, last)), acc)
        for side in range(2):
            acc = strip_taps(n, side, acc)
        return acc

    square = (chans, LANES)
    diagonal = iota(square, 0) == iota(square, 1)

    def to_lanes(values):
        return jnp.sum(jnp.where(diagonal, values, 0.0), axis=0, keepdims=True)

    def to_rows(values):
        spread = jnp.where(diagonal, jnp.broadcast_to(values, square), 0.0)
        return jnp.broadcast_to(jnp.sum(spread, axis=1, keepdims=True), square)

    def merge(own, other, size, stats, sends, recvs, n, axis_size, along_row):
        base = n * axis_size
        stats[base, pl.ds(0, 1), :] = own
        stats[base, pl.ds(1, 1), :] = other
        copies = []
        for d in range(1, axis_size):
            device = (
                (lax.rem(row + d, axis_size), col)
                if along_row
                else (row, lax.rem(col + d, axis_size))
            )
            copy = remote(
                stats.at[base],
                stats.at[base + d],
                sends.at[base + d],
                recvs.at[base + d],
                device,
            )
            copy.start()
            copies.append(copy)
        if n == 0 and not along_row:
            band(1, second_ref)
        for copy in copies:
            copy.wait()
        means = [stats[base + d, pl.ds(0, 1), :] for d in range(axis_size)]
        mean = sum(means) / axis_size
        squares = sum(stats[base + d, pl.ds(1, 1), :] for d in range(axis_size))
        spread = sum((m - mean) * (m - mean) for m in means)
        return mean, squares + size * spread

    def norm(acc, n, gain, shift):
        own = jnp.broadcast_to(jnp.sum(acc, axis=1, keepdims=True) / cells, square)
        across = jnp.concatenate([own] * GROUP, axis=0)
        squares = jnp.zeros(square, F32)
        for phase in range(phases):
            for g in range(count // GROUP):
                low = g * GROUP * chans
                at = pl.ds(phase * depth + low, GROUP * chans)
                for k in range(tiles):
                    cell = hidden[k, at, :]
                    for side, tile, start in ((0, 0, 0), (1, tiles - 1, edge)):
                        if k == tile:
                            moved = pltpu.roll(
                                edges[side, pl.ds(low, GROUP * chans), :],
                                (start - phase * STEP) % LANES,
                                1,
                            )
                            wanted = lanes >= edge if side else lanes < STEP
                            cell = cell + jnp.where(wanted, moved, 0.0)
                            hidden[k, at, :] = cell
                    diff = cell - across
                    diff = (diff * diff).reshape(GROUP, chans, LANES)
                    squares = squares + jnp.sum(diff, axis=0)
        squares = jnp.broadcast_to(jnp.sum(squares, axis=1, keepdims=True), square)
        mean, squares = merge(
            to_lanes(own), to_lanes(squares), cells, col_stats, cs_send, cs_recv, n, cols, False
        )
        mean, squares = merge(
            mean, squares, cells * cols, row_stats, rs_send, rs_recv, n, rows, True
        )
        blank = jnp.zeros((1, LANES - chans), F32)
        gains = jnp.concatenate([gain[...], blank], axis=1)
        shifts = jnp.concatenate([shift[...], blank], axis=1)
        factor = gains * lax.rsqrt(squares / (cells * (rows * cols)) + EPSILON)
        repeat = lambda v: jnp.concatenate([to_rows(v)] * (width // LANES), axis=1)
        return repeat(mean), repeat(factor), repeat(shifts)

    halo_start(pad_one, 0, x_ref, 0)
    pad_one[:, pl.ds(chans, depth), :] = x_ref[...]
    band(0, first_ref)
    mean, factor, shift = norm(conv(pad_one, 0), 0, gain_one, shift_one)

    def activate(phase, carry):
        for q in range(count):
            cell = held(pl.ds(phase * depth + q * chans, chans))
            cell = jnp.maximum((cell - mean) * factor + shift, 0.0)
            pad_two[phase, pl.ds((q + 1) * chans, chans), :] = cell.astype(BF16)
        return carry

    lax.fori_loop(0, phases, activate, 0, unroll=2)
    halo_start(pad_two, 1, pad_two, chans)
    mean, factor, shift = norm(conv(pad_two, 1), 1, gain_two, shift_two)

    def direct(source_col, source_block):
        z, p = lax.rem(source_col, 4), lax.rem(source_block, 4)
        chosen = (z == p) & (lax.rem(source_col + source_block, 8) < 4)
        for a, b in DIRECT:
            chosen = chosen | ((z == a) & (p == b))
        return chosen

    mine = direct(col, block)

    def crosses(target):
        return (2 * col < cols) != (2 * target < cols)

    def passes(d, k):
        target = lax.rem(col + d, cols)
        straight_on = direct(col, target)
        if k == pieces - 1:
            straight_on = straight_on | crosses(target) | (part == ratio - 1)
        return jnp.logical_not(straight_on)

    def span_of(k):
        p, at, size = table[k]
        return p, pl.ds(at, size)

    def source(h, k):
        return summed.at[(h, *span_of(k))]

    def landing(e, k):
        return got.at[(*span_of(k), pl.ds(e * count, count))]

    def waypoint(slot, k):
        return relay.at[(slot, *span_of(k))]

    def straight(h, k):
        return remote(
            source(h, k),
            landing(part, k),
            send.at[h * pieces + k],
            recv.at[part * pieces + k],
            (ratio * col + h, block),
        )

    def arrive(e, k):
        return remote(
            landing(e, k),
            landing(e, k),
            send.at[e * pieces + k],
            recv.at[e * pieces + k],
            (row, col),
        )

    def first_leg(h, k):
        slot = (lax.rem(block - col + cols, cols) - 1) * ratio + part
        return remote(
            source(h, k),
            waypoint(slot, k),
            send.at[h * pieces + k],
            relay_recv.at[slot * pieces + k],
            (ratio * col + h, col),
        )

    def second_leg(d, e, k):
        slot = (d - 1) * ratio + e
        return remote(
            waypoint(slot, k),
            landing(e, k),
            relay_send.at[slot * pieces + k],
            recv.at[e * pieces + k],
            (row, lax.rem(col + d, cols)),
        )

    def issue(k):
        for h in range(ratio):
            goes = relays | mine
            if k == pieces - 1:
                goes = goes | crosses(block) | (h == ratio - 1)
            here = relays & (part == h)

            @pl.when(goes & jnp.logical_not(here))
            def _(h=h):
                straight(h, k).start()

            @pl.when(jnp.logical_not(goes))
            def _(h=h):
                first_leg(h, k).start()

    def finish(phase, carry):
        for q in range(count):
            at = pl.ds(phase * depth + q * chans, chans)
            cell = (held(at) - mean) * factor + shift
            cell = (x_ref[phase, pl.ds(q * chans, chans), :].astype(F32) + cell).astype(BF16)
            for h in range(ratio):
                for p in range(parts):
                    summed[h, p, phase, q] = cell[
                        p * PART : (p + 1) * PART, h * height : (h + 1) * height
                    ]
            keep(at, cell.astype(F32))
        return carry

    for k in of_part(0):
        _, at, size = table[k]
        lax.fori_loop(at, at + size, finish, 0)
        issue(k)
    for k in range(len(of_part(0)), pieces):
        issue(k)

    @pl.when(relays)
    def _():
        for h in range(ratio):

            @pl.when(part == h)
            def _(h=h):
                got[:, :, pl.ds(h * count, count)] = summed[h]

    def forward(k):
        for d in range(1, cols):

            @pl.when(passes(d, k))
            def _(d=d):
                for e in range(ratio):
                    slot = (d - 1) * ratio + e
                    remote(
                        waypoint(slot, k),
                        waypoint(slot, k),
                        relay_send.at[slot * pieces + k],
                        relay_recv.at[slot * pieces + k],
                        (row, col),
                    ).wait_recv()
                    second_leg(d, e, k).start()

    def drain(k):
        for h in range(ratio):

            @pl.when(jnp.logical_not(relays & (part == h)))
            def _(h=h):
                straight(h, k).wait_send()

    span = ratio * depth
    unit = one_hot(iota((height, height), 0) == iota((height, height), 1))
    for p in range(parts):

        @pl.when(relays)
        def _(p=p):
            for k in of_part(p):
                forward(k)

        if p > 0:
            for k in of_part(p - 1):
                drain(k)

        def collect(phase, carry, p=p):
            for q in range(ratio * count):
                wide[pl.ds(phase * span + q * chans + p * PART, PART), :] = got[
                    p, phase, q
                ].astype(F32)
            return carry

        for k in of_part(p):
            for e in range(ratio):

                @pl.when(jnp.logical_not(relays & (part == e)))
                def _(e=e, k=k):
                    arrive(e, k).wait_recv()

            _, at, size = table[k]
            lax.fori_loop(at, at + size, collect, 0)

        if p == parts - 1:
            for k in of_part(p)[:-2]:
                drain(k)

        def turn(c, carry):
            own = jnp.concatenate(
                [
                    held(pl.ds(q * chans + c, phases, stride=depth))
                    for q in range(count)
                ],
                axis=0,
            )
            other = jnp.concatenate(
                [
                    wide[pl.ds(q * chans + c, phases, stride=span), :]
                    for q in range(ratio * count)
                ],
                axis=0,
            )
            total = own + lax.dot_general(
                unit, other.astype(BF16), (((1,), (1,)), ((), ())), preferred_element_type=F32
            )
            out_ref[c] = (total * 0.5).astype(BF16)
            return carry

        lax.fori_loop(p * PART, (p + 1) * PART, turn, 0, unroll=4)

    for k in of_part(parts - 1)[-2:]:
        drain(k)

    @pl.when(relays)
    def _():
        for k in range(pieces):
            for d in range(1, cols):

                @pl.when(passes(d, k))
                def _(d=d, k=k):
                    for e in range(ratio):
                        second_leg(d, e, k).wait_send()


def run(rows, cols, features, first, second, scales):
    chans, height, width = features.shape
    count = height // STEP
    depth = count * chans
    ratio = rows // cols
    slots = (cols - 1) * ratio
    parts = chans // PART
    pieces = len(piece_table(parts))
    full = depth + 2 * chans
    x = jnp.transpose(features.reshape(chans, count, STEP, width), (2, 1, 0, 3))
    x = x.reshape(STEP, depth, width)
    scales = [v.reshape(1, chans) for v in scales]
    vmem = pl.BlockSpec(memory_space=pltpu.VMEM)
    dma = pltpu.SemaphoreType.DMA
    return pl.pallas_call(
        functools.partial(kernel, rows, cols),
        out_shape=jax.ShapeDtypeStruct(features.shape, BF16),
        in_specs=[vmem] * 7,
        out_specs=vmem,
        scratch_shapes=[
            pltpu.VMEM((STEP, full, width), BF16),
            pltpu.VMEM((STEP, full, width), BF16),
            pltpu.VMEM((width // LANES, STEP * depth, LANES), F32),
            pltpu.VMEM((2 * STEP, 2 * LANES, LANES), BF16),
            pltpu.VMEM((2, depth, LANES), F32),
            pltpu.VMEM((2, 3, GROUP * chans, (GROUP + 2) * chans), BF16),
            pltpu.VMEM((2, 2, depth // 2, LANES), BF16),
            pltpu.VMEM((2, 2, depth // 2 + 2 * chans, LANES), BF16),
            pltpu.VMEM((2 * cols, 2, LANES), F32),
            pltpu.VMEM((2 * rows, 2, LANES), F32),
            pltpu.VMEM((ratio, parts, STEP, count, PART, height), BF16),
            pltpu.VMEM((parts, STEP, ratio * count, PART, height), BF16),
            pltpu.VMEM((STEP * ratio * depth, height), F32),
            pltpu.VMEM((slots, parts, STEP, count, PART, height), BF16),
            dma((16,)),
            dma((16,)),
            dma((2 * cols,)),
            dma((2 * cols,)),
            dma((2 * rows,)),
            dma((2 * rows,)),
            dma((ratio * pieces,)),
            dma((ratio * pieces,)),
            dma((slots * pieces,)),
            dma((slots * pieces,)),
        ],
        compiler_params=pltpu.CompilerParams(
            collective_id=0, has_side_effects=True, vmem_limit_bytes=44 * 1024 * 1024
        ),
    )(x, first, second, *scales)


def solution(mesh):
    rows, cols = mesh.shape["row"], mesh.shape["col"]

    def per_device(features, first, second, gain_one, shift_one, gain_two, shift_two):
        scales = (gain_one, shift_one, gain_two, shift_two)
        return run(rows, cols, features, first, second, scales)

    placed = (P(None, "row", "col"), P(), P(), P(), P(), P(), P())
    return jax.shard_map(
        per_device, mesh=mesh, in_specs=placed, out_specs=P(None, "row", "col"), check_vma=False
    )
```
